256 devices in a mesh: layer: 16 (over y, x), tx: 8 (over z), ty: 2 (over core).
Axes of the slice: x: 4, y: 4, z: 8, core: 2. Of those that a mesh axis runs over, the one named last changes fastest.
Arguments:
- krylov_block: float32 [4, 3, 128, 256, 256], P(None, None, 'layer', 'tx', 'ty'), may hold values from -1500 to 1500
- weights: float32 [3, 128, 256, 256], P(None, 'layer', 'tx', 'ty'), may hold values from 0.3 to 1.2
- pivots: float32 [128, 256, 256], P('layer', 'tx', 'ty'), may hold values from 0.015625 to 0.0625
- lower_ratio: float32 [128, 256, 256], P('layer', 'tx', 'ty'), may hold values from 0 to 1
- upper_ratio: float32 [128, 256, 256], P('layer', 'tx', 'ty'), may hold values from 0 to 1
- block_diag: float32 [9, 128, 256, 256], P(None, 'layer', 'tx', 'ty'), may hold values from -4 to 4
- block_inv: float32 [9, 128, 256, 256], P(None, 'layer', 'tx', 'ty'), may hold values from -4 to 4
- face_coef: float32 [6, 128, 256, 256], P(None, 'layer', 'tx', 'ty'), may hold values from 0.1 to 1
- fault_send_rows: int32 [16, 8, 2, 16, 8], P('layer', 'tx', 'ty'), may hold values from 0 to 255
- fault_recv_rows: int32 [16, 8, 2, 16, 8], P('layer', 'tx', 'ty'), may hold values from 0 to 255
- fault_counts: int32 [16, 8, 2, 16], P('layer', 'tx', 'ty'), may hold values from 0 to 8, as said below
- fault_coef: float32 [16, 8, 2, 16, 8, 128], P('layer', 'tx', 'ty'), may hold values from 0.2 to 1
- well_cells: int32 [8, 2, 16], P('tx', 'ty'), may hold values from 0 to 4095
- well_perfs: int32 [8, 2, 16, 8], P('tx', 'ty'), may hold values from 0 to 127
- well_index: float32 [8, 2, 16, 8], P('tx', 'ty'), may hold values from 0.5 to 2
Outputs:
- q_block: float32 [4, 3, 128, 256, 256], P(None, None, 'layer', 'tx', 'ty')
- r_factor: float32 [4, 4], replicated
The draws below stay inside these ranges and needn't reach their ends.
Inputs may be any that keep to these rules, and one draw needn't show every extreme that they name: `fault_counts`: in every group of tiles at one index of layer, at least one tile receives 8 rows from every source tile.
All inputs are finite; a program needn't handle non-finite values.
Results may differ from the reference program's by a relative error of at most 0.0003.
Values sent between devices are 32-bit elements; how exact they have to be, the bound alone decides.
No kernel may reach another device: no remote copies, remote signals or barrier semaphores. Data moves between devices by JAX's collectives and lax.ppermute only.
A program may use at most 128 MiB of HBM per device.

```python
import math
import jax
import jax.numpy as jnp
from jax import lax

LZ = 8
CX = 32
CY = 128
S = 4
CAP = 8
NW = 16
NP = 8
VERTICAL_TIERS = 128
LONGITUDE_SPAN = 256
LATITUDE_SPAN = 256
NT = 16
N_LAYER = 16
N_TX = 8
N_TY = 2


def draw_krylov_block(key, part):
    generator_starters = jax.random.split(key, 3)
    shape = (S, 3, VERTICAL_TIERS, LONGITUDE_SPAN, LATITUDE_SPAN)
    base = jnp.clip(jax.random.normal(generator_starters[0], shape, jnp.float32), -5.0, 5.0)
    depth = jnp.exp(jnp.log(3.0) * jnp.arange(VERTICAL_TIERS, dtype=jnp.float32) / VERTICAL_TIERS).reshape(1, 1, VERTICAL_TIERS, 1, 1)
    rowscale = jnp.exp(jnp.log(10.0) * jax.random.uniform(generator_starters[1], (1, 1, VERTICAL_TIERS, LONGITUDE_SPAN, 1), jnp.float32))
    colscale = jnp.exp(jnp.log(10.0) * jax.random.uniform(generator_starters[2], (S, 1, 1, 1, 1), jnp.float32))
    return base * depth * rowscale * colscale


def chain_ratio(key):
    generator_starters = jax.random.split(key, 5)
    share = 0.5
    slowly = jax.random.uniform(generator_starters[0], (1, LONGITUDE_SPAN, LATITUDE_SPAN), jnp.float32) < share
    keeping = jax.random.uniform(generator_starters[1], (1, LONGITUDE_SPAN, LATITUDE_SPAN), jnp.float32, 0.3, 0.8)
    slow_rate = jnp.exp(jnp.log(keeping) / VERTICAL_TIERS)
    lengths = jax.random.uniform(generator_starters[2], (1, LONGITUDE_SPAN, LATITUDE_SPAN), jnp.float32, 30.0, 50.0)
    fast_rate = jnp.exp(-1.0 / lengths)
    injected_fluid_amounts = jnp.where(slowly, slow_rate, fast_rate)
    abrupt_jumps = jax.random.uniform(generator_starters[3], (VERTICAL_TIERS, 1, 1), jnp.float32) < 2.0 / VERTICAL_TIERS
    misfit_terms = jax.random.uniform(generator_starters[4], (VERTICAL_TIERS, 1, 1), jnp.float32, 0.5, 0.8)
    return injected_fluid_amounts * jnp.where(abrupt_jumps, misfit_terms, 1.0)


def draw_lower_ratio(key, part):
    return chain_ratio(jax.random.fold_in(key, 11))


def draw_upper_ratio(key, part):
    return chain_ratio(jax.random.fold_in(key, 23))


def draw_fault_counts(key, part):
    generator_starters = jax.random.split(key, 3)
    light = jax.random.randint(generator_starters[0], (N_LAYER, N_TX, N_TY, NT), 0, CAP // 2 + 1)
    lucky = jax.random.randint(generator_starters[1], (N_LAYER, N_TX, N_TY, 1), 0, 4) == 0
    chosen = jax.random.randint(generator_starters[2], (N_LAYER, 1, 1, 1), 0, NT)
    number = (jnp.arange(N_TX)[:, None] * N_TY + jnp.arange(N_TY)[None, :]).reshape(1, N_TX, N_TY, 1)
    heavy = lucky | (number == chosen)
    return jnp.where(heavy, CAP, light).astype(jnp.int32)


def plant(values, key, smallest, high):
    spot = [jax.random.randint(jax.random.fold_in(key, axis), (), 0, length) for axis, length in enumerate(values.shape)]
    widest = values.shape.index(max(values.shape))
    neighbour = spot[:widest] + [(spot[widest] + 1) % values.shape[widest]] + spot[widest + 1:]
    return values.at[tuple(spot)].set(smallest).at[tuple(neighbour)].set(high)


def shard_levels(rng, extent, cuts, low, largest):
    factor_of = 1.0
    for position, shards_of in cuts:
        draws = jax.random.uniform(jax.random.fold_in(jax.random.fold_in(rng, 6), position), (shards_of,), jnp.float32, low / len(cuts), largest / len(cuts))
        factor_of = factor_of * jnp.repeat(jnp.exp(draws), extent[position] // shards_of).reshape((-1,) + (1,) * (len(extent) - 1 - position))
    return factor_of


def gaussian(stream_key, extent, width, most, cuts=(), held_as=jnp.bfloat16):
    array = jax.random.normal(stream_key, extent, jnp.float32) * width
    if len(cuts) > 0:
        array = shard_levels(stream_key, extent, cuts, -0.22, 0.18) * array
    return jnp.clip(array, min=-most, max=most).astype(held_as)


def setup_inputs(seed: int = 0) -> dict:
    keys = jax.random.split(jax.random.key(seed), 16)
    return {
        "krylov_block": draw_krylov_block(jax.random.fold_in(keys[15], 71), 0),
        "weights": jnp.clip(0.3 + 0.90000004 * jax.random.uniform(keys[1], (3, VERTICAL_TIERS, LONGITUDE_SPAN, LATITUDE_SPAN), jnp.float32) ** shard_levels(keys[1], (3, VERTICAL_TIERS, LONGITUDE_SPAN, LATITUDE_SPAN), ((1, 16), (2, 8), (3, 2)), -0.2, 0.2), 0.3, 1.2),
        "pivots": jnp.clip(jnp.exp(math.log(0.0625) - 1.3862944 * jax.random.uniform(keys[2], (VERTICAL_TIERS, LONGITUDE_SPAN, LATITUDE_SPAN), jnp.float32) ** shard_levels(keys[2], (VERTICAL_TIERS, LONGITUDE_SPAN, LATITUDE_SPAN), ((0, 16), (1, 8), (2, 2)), -0.2, 0.2)), 0.015625, 0.0625),
        "lower_ratio": draw_lower_ratio(jax.random.fold_in(keys[15], 71), 0),
        "upper_ratio": draw_upper_ratio(jax.random.fold_in(keys[15], 71), 0),
        "block_diag": gaussian(keys[5], (9, VERTICAL_TIERS, LONGITUDE_SPAN, LATITUDE_SPAN), 1.0, 4.0, ((1, 16), (2, 8), (3, 2)), jnp.float32),
        "block_inv": gaussian(keys[6], (9, VERTICAL_TIERS, LONGITUDE_SPAN, LATITUDE_SPAN), 0.5, 4.0, ((1, 16), (2, 8), (3, 2)), jnp.float32),
        "face_coef": jnp.clip(0.1 + 0.9 * jax.random.uniform(keys[7], (6, VERTICAL_TIERS, LONGITUDE_SPAN, LATITUDE_SPAN), jnp.float32) ** shard_levels(keys[7], (6, VERTICAL_TIERS, LONGITUDE_SPAN, LATITUDE_SPAN), ((1, 16), (2, 8), (3, 2)), -0.2, 0.2), 0.1, 1.0),
        "fault_send_rows": plant(jax.random.randint(keys[8], (N_LAYER, N_TX, N_TY, NT, CAP), 0, LZ * CX), jax.random.fold_in(keys[8], 1), 0, (LZ * CX) - 1).astype(jnp.int32),
        "fault_recv_rows": plant(jax.random.randint(keys[9], (N_LAYER, N_TX, N_TY, NT, CAP), 0, LZ * CX), jax.random.fold_in(keys[9], 1), 0, (LZ * CX) - 1).astype(jnp.int32),
        "fault_counts": draw_fault_counts(jax.random.fold_in(keys[15], 71), 0),
        "fault_coef": jnp.clip(0.2 + 0.8 * jax.random.uniform(keys[11], (N_LAYER, N_TX, N_TY, NT, CAP, CY), jnp.float32) ** shard_levels(keys[11], (N_LAYER, N_TX, N_TY, NT, CAP, CY), ((0, 16), (1, 8), (2, 2)), -0.2, 0.2), 0.2, 1.0),
        "well_cells": plant(jax.random.randint(keys[12], (N_TX, N_TY, NW), 0, CX * CY), jax.random.fold_in(keys[12], 1), 0, (CX * CY) - 1).astype(jnp.int32),
        "well_perfs": plant(jax.random.randint(keys[13], (N_TX, N_TY, NW, NP), 0, VERTICAL_TIERS), jax.random.fold_in(keys[13], 1), 0, VERTICAL_TIERS - 1).astype(jnp.int32),
        "well_index": jnp.clip(jnp.exp(math.log(2.0) - 1.3862944 * jax.random.uniform(keys[14], (N_TX, N_TY, NW, NP), jnp.float32) ** shard_levels(keys[14], (N_TX, N_TY, NW, NP), ((0, 8), (1, 2)), -0.2, 0.2)), 0.5, 2.0),
    }


HIGH = lax.Precision.HIGHEST

def mix(matrix, vectors):
    return matrix[None, :, 0] * vectors[:, 0:1] + matrix[None, :, 1] * vectors[:, 1:2] + matrix[None, :, 2] * vectors[:, 2:3]

def apply_stencil(values, padded, blocks, faces):
    result = mix(blocks, values)
    beside = [padded[:, :, :-2, 1:-1, 1:-1], padded[:, :, 2:, 1:-1, 1:-1], padded[:, :, 1:-1, :-2, 1:-1], padded[:, :, 1:-1, 2:, 1:-1], padded[:, :, 1:-1, 1:-1, :-2], padded[:, :, 1:-1, 1:-1, 2:]]
    for number in range(6):
        result = result - faces[number][None, None] * beside[number]
    return result

def reference(krylov_block, weights, pivots, lower_ratio, upper_ratio, block_diag, block_inv, face_coef, fault_send_rows, fault_recv_rows, fault_counts, fault_coef, well_cells, well_perfs, well_index):
    sources = jnp.sum(weights[None] * krylov_block, axis=1)
    start = jnp.zeros((S, LONGITUDE_SPAN, LATITUDE_SPAN), jnp.float32)

    def forward_step(level, inputs):
        pivot_row, ratio_row, source_row = inputs
        level = pivot_row[None] * source_row + ratio_row[None] * level
        return (level, level)
    _, upward = lax.scan(forward_step, start, (pivots, lower_ratio, jnp.moveaxis(sources, 1, 0)))

    def backward_step(level, inputs):
        ratio_row, source_row = inputs
        level = source_row + ratio_row[None] * level
        return (level, level)
    _, pressure = lax.scan(backward_step, start, (upper_ratio, upward), reverse=True)
    pressure = jnp.moveaxis(pressure, 0, 1)
    blocks = block_diag.reshape(3, 3, VERTICAL_TIERS, LONGITUDE_SPAN, LATITUDE_SPAN)
    inverse = block_inv.reshape(3, 3, VERTICAL_TIERS, LONGITUDE_SPAN, LATITUDE_SPAN)
    residue = krylov_block - blocks[None, :, 0] * pressure[:, None]
    precond = mix(inverse, residue)
    precond = precond.at[:, 0].add(pressure)
    padded = jnp.pad(precond, ((0, 0), (0, 0), (1, 1), (1, 1), (1, 1)))
    image = apply_stencil(precond, padded, blocks, face_coef)
    tiles = N_TX * N_TY
    tile_rows = LZ * CX
    order = (0, 1, 2, 4, 6, 3, 5, 7)
    tiled = precond.reshape(S, 3, N_LAYER, LZ, N_TX, CX, N_TY, CY).transpose(order).reshape(S, 3, -1, CY)
    offsets = (jnp.arange(N_LAYER * tiles, dtype=jnp.int32) * tile_rows).reshape(N_LAYER, tiles, 1, 1)
    sender = fault_send_rows.reshape(N_LAYER, tiles, tiles, CAP) + offsets
    picked = jnp.take(tiled, sender.reshape(-1), axis=2).reshape(S, 3, N_LAYER, tiles, tiles, CAP, CY)
    picked = jnp.swapaxes(picked, 3, 4)
    live = (jnp.arange(CAP, dtype=jnp.int32)[None, None, None, :] < fault_counts.reshape(N_LAYER, tiles, tiles)[..., None]).astype(jnp.float32)
    weight_rows = fault_coef.reshape(N_LAYER, tiles, tiles, CAP, CY) * live[..., None]
    arrived = picked * weight_rows[None, None]
    target = (fault_recv_rows.reshape(N_LAYER, tiles, tiles, CAP) + offsets).reshape(-1)
    image_tiled = image.reshape(S, 3, N_LAYER, LZ, N_TX, CX, N_TY, CY).transpose(order).reshape(S, 3, -1, CY)
    image_tiled = image_tiled.at[:, :, target].add(-arrived.reshape(S, 3, -1, CY))
    image = image_tiled.reshape(S, 3, N_LAYER, N_TX, N_TY, LZ, CX, CY).transpose(0, 1, 2, 5, 3, 6, 4, 7)
    image = image.reshape(S, 3, VERTICAL_TIERS, LONGITUDE_SPAN, LATITUDE_SPAN)
    lateral_x = (jnp.arange(N_TX, dtype=jnp.int32)[:, None, None] * CX + well_cells // CY)[..., None]
    lateral_y = (jnp.arange(N_TY, dtype=jnp.int32)[None, :, None] * CY + well_cells % CY)[..., None]
    drawn = precond[:, 0][:, well_perfs, lateral_x, lateral_y]
    rates = jnp.sum(well_index[None] * drawn, axis=-1)
    added = well_index[None] * rates[..., None] / NP
    image_zero = image[:, 0].at[:, well_perfs, lateral_x, lateral_y].add(added)
    image = image.at[:, 0].set(image_zero)
    flat = image.reshape(S, -1)
    entries = 3.0 * VERTICAL_TIERS * LONGITUDE_SPAN * LATITUDE_SPAN
    gram = jnp.dot(flat, flat.T, precision=HIGH) / entries
    lower = jnp.linalg.cholesky(gram)
    q_flat = lax.linalg.triangular_solve(lower, flat, left_side=True, lower=True)
    return (q_flat.reshape(image.shape), lower.T)
```

```python
import jax
import jax.numpy as jnp
from jax import lax
from jax.experimental import pallas as pl
from jax.experimental.pallas import tpu as pltpu
from jax.sharding import PartitionSpec as P

F32 = jnp.float32
COLS, COMPS, LAYERS, XS, LANES = 4, 3, 8, 32, 128
BLOCKS = XS // 8
PLANE = LAYERS * XS
TILES, SLOTS = 16, 8
CHUNKS = 16
MSG = 24
WELLS, PERFS = 16, 8
ALL = ("layer", "tx", "ty")


def iota(shape, dim):
    return lax.broadcasted_iota(jnp.int32, shape, dim)


def rows_at(plane, layer, block):
    return pl.ds(plane * PLANE + layer * XS + block * 8, 8)


def chunk_rows(row, block):
    return pl.ds(MSG * 8 * (block % 2) + row + block // 2, 8, stride=MSG)


def sweep_kernel(
    ids, cells, perfs, index, krylov, weights, pivots, lower, upper, diag0, diag3, diag6, inv,
    message, base, from_below, from_above, well_weights, drawn,
):
    for block in range(BLOCKS):
        levels = [[] for _ in range(COLS)]
        products = []
        for k in range(LAYERS):
            at = rows_at(0, k, block)
            restrict = [weights[rows_at(c, k, block), :] for c in range(COMPS)]
            pivot = pivots[at, :]
            ratio = lower[at, :]
            products.append(ratio if k == 0 else ratio * products[-1])
            for s in range(COLS):
                source = restrict[0] * krylov[rows_at(s * 3, k, block), :]
                source += restrict[1] * krylov[rows_at(s * 3 + 1, k, block), :]
                source += restrict[2] * krylov[rows_at(s * 3 + 2, k, block), :]
                level = pivot * source
                levels[s].append(level if k == 0 else level + ratio * levels[s][-1])
        for s in range(COLS):
            message[chunk_rows(2 * s, block), :] = levels[s][-1]
        message[chunk_rows(16, block), :] = products[-1]
        down = [None] * COLS
        low = high = None
        for k in reversed(range(LAYERS)):
            at = rows_at(0, k, block)
            ratio = upper[at, :]
            first = k == LAYERS - 1
            low = products[k] if first else products[k] + ratio * low
            high = ratio if first else ratio * high
            from_below[at, :] = low
            from_above[at, :] = high
            inverse = [inv[rows_at(c, k, block), :] for c in range(COMPS)]
            share = 1.0 - (
                inverse[0] * diag0[at, :] + inverse[1] * diag3[at, :] + inverse[2] * diag6[at, :]
            )
            drawn[rows_at(4, k, block), :] = share * low
            drawn[rows_at(5, k, block), :] = share * high
            for s in range(COLS):
                down[s] = levels[s][k] if first else levels[s][k] + ratio * down[s]
                base[rows_at(s, k, block), :] = down[s]
                value = inverse[0] * krylov[rows_at(s * 3, k, block), :]
                value += inverse[1] * krylov[rows_at(s * 3 + 1, k, block), :]
                value += inverse[2] * krylov[rows_at(s * 3 + 2, k, block), :]
                drawn[rows_at(s, k, block), :] = value + share * down[s]
        for s in range(COLS):
            message[chunk_rows(8 + 2 * s, block), :] = down[s]
        message[chunk_rows(18, block), :] = high
        message[chunk_rows(20, block), :] = low
    sub, lane = iota((8, LANES), 0), iota((8, LANES), 1)
    first_layer = ids[0, 0] * LAYERS
    total = jnp.zeros((8, LANES), F32)
    for w in range(WELLS):
        cell = cells[0, w]
        x, y = lax.shift_right_logical(cell, 7), cell & 127
        strength = jnp.zeros((8, LANES), F32)
        for p in range(PERFS):
            strength += jnp.where(sub == perfs[w, p] - first_layer, index[w, p], 0.0)
        well_weights[pl.ds(w * 8, 8), :] = strength
        picked = jnp.where(lane == y, strength, 0.0)
        for q in range(6):
            value = drawn[pl.ds(q * PLANE + x, 8, stride=XS), :] * picked
            total += pltpu.roll(value, (q * WELLS + w + LANES - y) & 127, 1)
    row = jnp.sum(total, axis=0, keepdims=True)
    message[pl.ds(22, CHUNKS, stride=MSG), :] = jnp.broadcast_to(row, (CHUNKS, LANES))
    message[pl.ds(23, CHUNKS, stride=MSG), :] = jnp.zeros((CHUNKS, LANES), F32)


def pick(matrix, chosen):
    high = matrix.astype(jnp.bfloat16)
    rest = matrix - high.astype(F32)
    middle = rest.astype(jnp.bfloat16)
    low = (rest - middle.astype(F32)).astype(jnp.bfloat16)
    chosen = chosen.astype(jnp.bfloat16)
    return (
        jnp.dot(high, chosen, preferred_element_type=F32)
        + jnp.dot(middle, chosen, preferred_element_type=F32)
        + jnp.dot(low, chosen, preferred_element_type=F32)
    )


def chain_kernel(ids, cells, message, reply, states):
    sub, lane = iota((8, LANES), 0), iota((8, LANES), 1)

    def spread(rows, first):
        pair = pltpu.roll(rows, (8 - first) % 8, 0) if first else rows
        pair = jnp.where(sub < 2, pair, 0.0)
        pair += pltpu.roll(pair, 2, 0)
        return pair + pltpu.roll(pair, 4, 0)

    tails = [message[pl.ds(l * MSG + 16, 8), :] for l in range(CHUNKS)]
    state = jnp.zeros((8, LANES), F32)
    entering = []
    for l in range(CHUNKS):
        entering.append(state)
        reply[pl.ds(l * MSG, 8), :] = state
        states[pl.ds(l * 8, 8), pl.ds(0, LANES)] = state
        if l < CHUNKS - 1:
            state = message[pl.ds(l * MSG, 8), :] + spread(tails[l], 0) * state
    state = jnp.zeros((8, LANES), F32)
    for l in reversed(range(CHUNKS)):
        reply[pl.ds(l * MSG + 8, 8), :] = state
        states[pl.ds(l * 8, 8), pl.ds(LANES, LANES)] = state
        if l > 0:
            state = (
                message[pl.ds(l * MSG + 8, 8), :]
                + spread(tails[l], 4) * entering[l]
                + spread(tails[l], 2) * state
            )
    me = ids[0, 0]
    wide = (2 * LANES, 2 * LANES)
    col = iota((1, 2 * LANES), 1)
    owner = jnp.zeros((1, 2 * LANES), jnp.int32)
    for w in range(WELLS):
        owner = jnp.where((col & 15) == w, cells[0, w], owner)
    line, column = iota(wide, 0), iota(wide, 1)
    place = (lax.shift_right_logical(column, 7) * 16 + me) * LANES + (line & 127)
    group = lax.shift_right_logical(column & 127, 4) - 4
    chosen = jnp.where(
        (jnp.broadcast_to(owner, wide) == place) & (group == lax.shift_right_logical(line, 7)),
        1.0,
        0.0,
    )
    found = pick(states[...], chosen)
    odd = (sub & 1) == 1
    total = jnp.zeros((8, LANES), F32)
    fixed = jnp.zeros((1, LANES), F32)
    for l in range(CHUNKS):
        row = tails[l][6:7, :]
        fixed += row
        here = found[l * 8 : l * 8 + 8, :]
        total += row * jnp.where(odd, here[:, LANES:], here[:, :LANES])
    rates = pltpu.roll(total, 64, 1) + pltpu.roll(total, 48, 1)
    fixed = jnp.broadcast_to(jnp.where(me == 0, fixed, 0.0), (8, LANES))
    for s in range(COLS):
        mine = fixed if s == 0 else pltpu.roll(fixed, LANES - 16 * s, 1)
        rates += jnp.where(sub == 2 * s, mine, 0.0)
    rates = jnp.where(lane < WELLS, rates, 0.0)
    for l in range(CHUNKS):
        reply[pl.ds(l * MSG + 16, 8), :] = rates


def precond_kernel(
    ids, send_rows, reply, base, from_below, from_above, krylov, diag0, diag3, diag6, inv,
    precond, x_a, x_b, layer_a, layer_b, outgoing, rates,
):
    for block in range(BLOCKS):
        below = [reply[chunk_rows(2 * s, block), :] for s in range(COLS)]
        above = [reply[chunk_rows(8 + 2 * s, block), :] for s in range(COLS)]
        for k in range(LAYERS):
            at = rows_at(0, k, block)
            low, high = from_below[at, :], from_above[at, :]
            diag = [diag0[at, :], diag3[at, :], diag6[at, :]]
            inverse = [inv[rows_at(e, k, block), :] for e in range(9)]
            for s in range(COLS):
                pressure = base[rows_at(s, k, block), :] + low * below[s] + high * above[s]
                residue = [
                    krylov[rows_at(s * 3 + c, k, block), :] - diag[c] * pressure
                    for c in range(COMPS)
                ]
                for c in range(COMPS):
                    value = (
                        inverse[3 * c] * residue[0]
                        + inverse[3 * c + 1] * residue[1]
                        + inverse[3 * c + 2] * residue[2]
                    )
                    precond[rows_at(s * 3 + c, k, block), :] = value + pressure if c == 0 else value
    layer_even = (ids[0, 0] & 1) == 0
    x_even = (ids[0, 1] & 1) == 0
    x_a[...] = precond[pl.ds(jnp.where(x_even, XS - 1, 0), 96, stride=XS), :]
    x_b[...] = precond[pl.ds(jnp.where(x_even, 0, XS - 1), 96, stride=XS), :]
    layer_first = pl.multiple_of(jnp.where(layer_even, (LAYERS - 1) * XS, 0), XS)
    layer_second = pl.multiple_of(jnp.where(layer_even, 0, (LAYERS - 1) * XS), XS)
    for plane in range(12):
        layer_a[pl.ds(plane * XS, XS), :] = precond[pl.ds(plane * PLANE + layer_first, XS), :]
        layer_b[pl.ds(plane * XS, XS), :] = precond[pl.ds(plane * PLANE + layer_second, XS), :]
    for u in range(TILES):
        for j in range(SLOTS):
            row = send_rows[u, j]
            outgoing[pl.ds(u * 96 + j * 8, 8), :] = precond[pl.ds(row, 8, stride=PLANE), :]
            outgoing[pl.ds(u * 96 + 64 + j * 4, 4), :] = precond[
                pl.ds(row + 8 * PLANE, 4, stride=PLANE), :
            ]
    total = reply[pl.ds(16, 8), :]
    for j in range(1, CHUNKS):
        total += reply[pl.ds(j * MSG + 16, 8), :]
    rates[...] = total


def image_kernel(
    ids, cells, recv_rows, counts, precond, across, x_a, x_b, layer_a, layer_b, arrived, coef,
    diag, faces, rates, well_weights, image, gram,
):
    sub, lane = iota((8, LANES), 0), iota((8, LANES), 1)
    layer_even = (ids[0, 0] & 1) == 0
    x_even = (ids[0, 1] & 1) == 0
    y_first = ids[0, 2] == 0
    image[...] = jnp.zeros(image.shape, F32)
    for u in range(TILES):
        for j in range(SLOTS):
            row = recv_rows[u, j]
            slot = u * SLOTS + j
            weight = jnp.where(j < counts[0, u], coef[pl.ds(slot, 1), :], 0.0)
            image[pl.ds(row, 8, stride=PLANE), :] -= weight * arrived[pl.ds(u * 96 + j * 8, 8), :]
            image[pl.ds(row + 8 * PLANE, 4, stride=PLANE), :] -= (
                weight * arrived[pl.ds(u * 96 + 64 + j * 4, 4), :]
            )
    rate = rates[...]
    rate = (rate + pltpu.roll(rate, 7, 0)) * (1.0 / PERFS)
    for w in range(WELLS):
        cell = cells[0, w]
        x, y = lax.shift_right_logical(cell, 7), cell & 127
        strength = well_weights[pl.ds(w * 8, 8), :]
        placed = pltpu.roll(jnp.where(lane == w, rate, 0.0), (y + LANES - w) & 127, 1)
        for s in range(COLS):
            image[pl.ds(s * 3 * PLANE + x, 8, stride=XS), :] += strength * placed[2 * s : 2 * s + 1, :]
    sums = {}
    row_x = iota((XS, LANES), 0)
    lane_y = iota((XS, LANES), 1)

    def column(k, _):
        def at(plane, size=XS, layer=None):
            layer = k if layer is None else layer
            return pl.ds(pl.multiple_of(plane * PLANE + layer * XS, XS), size)

        totals = list(_)
        blocks = [diag[at(e), :] for e in range(9)]
        face = [faces[at(f), :] for f in range(6)]
        images = []
        for s in range(COLS):
            value = [precond[at(s * 3 + c), :] for c in range(COMPS)]
            for c in range(COMPS):
                plane = s * 3 + c
                here = value[c]
                out = image[at(plane), :]
                out += blocks[3 * c] * value[0]
                out += blocks[3 * c + 1] * value[1]
                out += blocks[3 * c + 2] * value[2]
                edge = pl.ds(plane * XS, XS)
                inner = precond[at(plane, layer=jnp.maximum(k - 1, 0)), :]
                outer = jnp.where(layer_even, layer_b[edge, :], layer_a[edge, :])
                out -= face[0] * jnp.where(k == 0, outer, inner)
                inner = precond[at(plane, layer=jnp.minimum(k + 1, LAYERS - 1)), :]
                outer = jnp.where(layer_even, layer_a[edge, :], layer_b[edge, :])
                out -= face[1] * jnp.where(k == LAYERS - 1, outer, inner)
                side = pl.ds(plane * LAYERS + k, 1)
                first, second = x_a[side, :], x_b[side, :]
                outer = jnp.where(x_even, second, first)
                out -= face[2] * jnp.where(row_x == 0, outer, pltpu.roll(here, 1, 0))
                outer = jnp.where(x_even, first, second)
                out -= face[3] * jnp.where(row_x == XS - 1, outer, pltpu.roll(here, XS - 1, 0))
                other = across[at(plane), :]
                edge_low = jnp.where(y_first, 0.0, other)
                edge_high = jnp.where(y_first, other, 0.0)
                out -= face[4] * pltpu.roll(jnp.where(lane_y == LANES - 1, edge_low, here), 1, 1)
                out -= face[5] * pltpu.roll(jnp.where(lane_y == 0, edge_high, here), LANES - 1, 1)
                image[at(plane), :] = out
                images.append(out)
        n = 0
        for s in range(COLS):
            for t in range(s + 1):
                value = images[s * 3] * images[t * 3]
                value += images[s * 3 + 1] * images[t * 3 + 1]
                value += images[s * 3 + 2] * images[t * 3 + 2]
                totals[n] += jnp.sum(value.reshape(BLOCKS, 8, LANES), axis=0)
                n += 1
        return tuple(totals)

    sums = lax.fori_loop(
        0, LAYERS, column, tuple(jnp.zeros((8, LANES), F32) for _ in range(10))
    )
    packed = jnp.zeros((1, LANES), F32)
    lanes = iota((1, LANES), 1)
    for n in range(10):
        value = jnp.sum(jnp.sum(sums[n], axis=0, keepdims=True), axis=1, keepdims=True)
        packed = jnp.where(lanes == n, value, packed)
    gram[...] = jnp.broadcast_to(packed, gram.shape)


def factor_kernel(scale, gathered, image, q, factor):
    total = jnp.sum(gathered[...].reshape(-1, 8, LANES), axis=0)
    total = jnp.sum(total, axis=0, keepdims=True) * scale
    lanes = iota((1, LANES), 1)
    entry, n = {}, 0
    for s in range(COLS):
        for t in range(s + 1):
            entry[s, t] = jnp.sum(jnp.where(lanes == n, total, 0.0), axis=1, keepdims=True)
            n += 1
    lower = {}
    for t in range(COLS):
        value = entry[t, t]
        for i in range(t):
            value -= lower[t, i] * lower[t, i]
        lower[t, t] = jnp.sqrt(value)
        for s in range(t + 1, COLS):
            value = entry[s, t]
            for i in range(t):
                value -= lower[s, i] * lower[t, i]
            lower[s, t] = value / lower[t, t]
    line, col = iota((COLS, COLS), 0), iota((COLS, COLS), 1)
    result = jnp.zeros((COLS, COLS), F32)
    for (s, t), value in lower.items():
        result = jnp.where((line == t) & (col == s), value, result)
    factor[...] = result
    wide = {key: jnp.broadcast_to(value, (8, LANES)) for key, value in lower.items()}
    inverse = {t: 1.0 / wide[t, t] for t in range(COLS)}

    def step(i, _):
        at = pl.multiple_of(i * 8, 8)
        done = []
        for s in range(COLS):
            for_s = []
            for c in range(COMPS):
                value = image[pl.ds((s * 3 + c) * PLANE + at, 8), :]
                for t in range(s):
                    value -= wide[s, t] * done[t][c]
                value *= inverse[s]
                q[pl.ds((s * 3 + c) * PLANE + at, 8), :] = value
                for_s.append(value)
            done.append(for_s)
        return _

    lax.fori_loop(0, PLANE // 8, step, 0, unroll=4)


SMEM = pl.BlockSpec(memory_space=pltpu.SMEM)
VMEM = pl.BlockSpec(memory_space=pltpu.VMEM)


def part(plane, planes=1):
    return pl.BlockSpec((planes * PLANE, LANES), lambda i: (plane, 0))


def whole(rows):
    return pl.BlockSpec((rows, LANES), lambda i: (0, 0))


def shape(*rows):
    return tuple(jax.ShapeDtypeStruct((r, LANES), F32) for r in rows)


def call(kernel, name, outs, ins, smems=1, scratch=(), flops=1_000_000):
    def run(*args):
        specs = [SMEM] * smems
        for arg, spec in zip(args[smems:], ins, strict=True):
            specs.append(whole(arg.shape[0]) if spec is None else spec)
        size = sum(a.size * 4 for a in args)
        return pl.pallas_call(
            kernel,
            name=name,
            grid=(1,),
            out_shape=outs,
            in_specs=specs,
            out_specs=tuple(
                pl.BlockSpec(o.shape, lambda i: (0,) * len(o.shape)) for o in outs
            ),
            scratch_shapes=list(scratch),
            compiler_params=pltpu.CompilerParams(vmem_limit_bytes=28 << 20),
            cost_estimate=pl.CostEstimate(flops=flops, bytes_accessed=size, transcendentals=0),
        )(*args)

    return run


def pairs(size, odd):
    found = []
    for i in range(1 if odd else 0, size - 1, 2):
        found += [(i, i + 1), (i + 1, i)]
    return found


def on_device(
    krylov_block,
    weights,
    pivots,
    lower_ratio,
    upper_ratio,
    block_diag,
    block_inv,
    face_coef,
    fault_send_rows,
    fault_recv_rows,
    fault_counts,
    fault_coef,
    well_cells,
    well_perfs,
    well_index,
):
    n_layer, n_tx, n_ty = (lax.axis_size(a) for a in ALL)

    def flat(array):
        return array.reshape(-1, LANES)

    krylov, diag, inv, faces = (
        flat(a) for a in (krylov_block, block_diag, block_inv, face_coef)
    )
    ids = jnp.stack([lax.axis_index(a) for a in ALL]).astype(jnp.int32).reshape(1, 3)
    cells = well_cells.reshape(1, WELLS)
    perfs = well_perfs.reshape(WELLS, PERFS)
    index = well_index.reshape(WELLS, PERFS)
    send_rows = fault_send_rows.reshape(TILES, SLOTS)
    recv_rows = fault_recv_rows.reshape(TILES, SLOTS)
    counts = fault_counts.reshape(1, TILES)
    columns = (part(0), part(3), part(6))
    message, base, from_below, from_above, well_weights = call(
        sweep_kernel,
        "sweep",
        shape(CHUNKS * MSG, COLS * PLANE, PLANE, PLANE, WELLS * 8),
        (None,) * 5 + columns + (part(0, 3),),
        smems=4,
        scratch=(pltpu.VMEM((6 * PLANE, LANES), F32),),
    )(
        ids, cells, perfs, index, krylov, flat(weights), flat(pivots), flat(lower_ratio),
        flat(upper_ratio), diag, diag, diag, inv,
    )
    message = lax.all_to_all(
        message.reshape(CHUNKS, MSG, LANES), "layer", split_axis=0, concat_axis=0, tiled=True
    )
    (reply,) = call(
        chain_kernel,
        "chain",
        shape(CHUNKS * MSG),
        (None,),
        smems=2,
        scratch=(pltpu.VMEM((LANES, 2 * LANES), F32),),
    )(ids, cells, flat(message))
    reply = lax.all_to_all(
        reply.reshape(CHUNKS, MSG, LANES), "layer", split_axis=0, concat_axis=0, tiled=True
    )
    precond, x_a, x_b, layer_a, layer_b, outgoing, rates = call(
        precond_kernel,
        "precond",
        shape(12 * PLANE, 96, 96, 12 * XS, 12 * XS, TILES * 96, 8),
        (None,) * 5 + columns + (None,),
        smems=2,
    )(
        ids, send_rows, flat(reply), base, from_below, from_above, krylov, diag, diag, diag, inv
    )
    across = lax.ppermute(precond, "ty", pairs(n_ty, False))
    x_a = lax.ppermute(x_a, "tx", pairs(n_tx, False))
    x_b = lax.ppermute(x_b, "tx", pairs(n_tx, True))
    layer_a = lax.ppermute(layer_a, "layer", pairs(n_layer, False))
    layer_b = lax.ppermute(layer_b, "layer", pairs(n_layer, True))
    arrived = lax.all_to_all(
        outgoing.reshape(TILES, 96, LANES), ("tx", "ty"), split_axis=0, concat_axis=0, tiled=True
    )
    devices = n_layer * n_tx * n_ty
    image, gram = call(
        image_kernel,
        "image",
        shape(12 * PLANE, devices),
        (None,) * 12,
        smems=4,
    )(
        ids, cells, recv_rows, counts, precond, across, x_a, x_b, layer_a, layer_b, flat(arrived),
        flat(fault_coef), diag, faces, rates, well_weights,
    )
    gathered = lax.all_to_all(gram, ALL, split_axis=0, concat_axis=0, tiled=True)
    entries = float(12 * PLANE * LANES // COLS * devices)

    def factor(*refs):
        factor_kernel(1.0 / entries, *refs)

    q, r_factor = call(
        factor,
        "factor",
        shape(12 * PLANE) + (jax.ShapeDtypeStruct((COLS, COLS), F32),),
        (None, None),
        smems=0,
    )(gathered, image)
    return (q.reshape(krylov_block.shape), r_factor)


def solution(mesh):
    placed = (
        P(None, None, "layer", "tx", "ty"),
        P(None, "layer", "tx", "ty"),
        P("layer", "tx", "ty"),
        P("layer", "tx", "ty"),
        P("layer", "tx", "ty"),
        P(None, "layer", "tx", "ty"),
        P(None, "layer", "tx", "ty"),
        P(None, "layer", "tx", "ty"),
        P("layer", "tx", "ty", None, None),
        P("layer", "tx", "ty", None, None),
        P("layer", "tx", "ty", None),
        P("layer", "tx", "ty", None, None, None),
        P("tx", "ty", None),
        P("tx", "ty", None, None),
        P("tx", "ty", None, None),
    )
    return jax.shard_map(
        on_device,
        mesh=mesh,
        in_specs=placed,
        out_specs=(P(None, None, "layer", "tx", "ty"), P()),
        check_vma=False,
    )
```

```python
import jax
import jax.numpy as jnp
from jax import lax
from jax.experimental import pallas as pl
from jax.experimental.pallas import tpu as pltpu
from jax.sharding import PartitionSpec as P

F32 = jnp.float32
COLS, COMPS, LAYERS, XS, LANES = 4, 3, 8, 32, 128
BLOCKS = XS // 8
PLANE = LAYERS * XS
TILES, SLOTS = 16, 8
CHUNKS = 16
MSG = 24
WELLS, PERFS = 16, 8
ALL = ("layer", "tx", "ty")


def iota(shape, dim):
    return lax.broadcasted_iota(jnp.int32, shape, dim)


def rows_at(plane, layer, block):
    return pl.ds(plane * PLANE + layer * XS + block * 8, 8)


def chunk_rows(row, block):
    return pl.ds(MSG * 8 * (block % 2) + row + block // 2, 8, stride=MSG)


def sweep_kernel(
    ids, cells, perfs, index, krylov, weights, pivots, lower, upper, diag0, diag3, diag6, inv,
    message, base, from_below, from_above, well_weights, drawn,
):
    for block in range(BLOCKS):
        levels = [[] for _ in range(COLS)]
        products = []
        for k in range(LAYERS):
            at = rows_at(0, k, block)
            restrict = [weights[rows_at(c, k, block), :] for c in range(COMPS)]
            pivot = pivots[at, :]
            ratio = lower[at, :]
            products.append(ratio if k == 0 else ratio * products[-1])
            for s in range(COLS):
                source = restrict[0] * krylov[rows_at(s * 3, k, block), :]
                source += restrict[1] * krylov[rows_at(s * 3 + 1, k, block), :]
                source += restrict[2] * krylov[rows_at(s * 3 + 2, k, block), :]
                level = pivot * source
                levels[s].append(level if k == 0 else level + ratio * levels[s][-1])
        for s in range(COLS):
            message[chunk_rows(2 * s, block), :] = levels[s][-1]
        message[chunk_rows(16, block), :] = products[-1]
        down = [None] * COLS
        low = high = None
        for k in reversed(range(LAYERS)):
            at = rows_at(0, k, block)
            ratio = upper[at, :]
            first = k == LAYERS - 1
            low = products[k] if first else products[k] + ratio * low
            high = ratio if first else ratio * high
            from_below[at, :] = low
            from_above[at, :] = high
            inverse = [inv[rows_at(c, k, block), :] for c in range(COMPS)]
            share = 1.0 - (
                inverse[0] * diag0[at, :] + inverse[1] * diag3[at, :] + inverse[2] * diag6[at, :]
            )
            drawn[rows_at(4, k, block), :] = share * low
            drawn[rows_at(5, k, block), :] = share * high
            for s in range(COLS):
                down[s] = levels[s][k] if first else levels[s][k] + ratio * down[s]
                base[rows_at(s, k, block), :] = down[s]
                value = inverse[0] * krylov[rows_at(s * 3, k, block), :]
                value += inverse[1] * krylov[rows_at(s * 3 + 1, k, block), :]
                value += inverse[2] * krylov[rows_at(s * 3 + 2, k, block), :]
                drawn[rows_at(s, k, block), :] = value + share * down[s]
        for s in range(COLS):
            message[chunk_rows(8 + 2 * s, block), :] = down[s]
        message[chunk_rows(18, block), :] = high
        message[chunk_rows(20, block), :] = low
    sub, lane = iota((8, LANES), 0), iota((8, LANES), 1)
    first_layer = ids[0, 0] * LAYERS
    total = jnp.zeros((8, LANES), F32)
    for w in range(WELLS):
        cell = cells[0, w]
        x, y = lax.shift_right_logical(cell, 7), cell & 127
        strength = jnp.zeros((8, LANES), F32)
        for p in range(PERFS):
            strength += jnp.where(sub == perfs[p, w] - first_layer, index[p, w], 0.0)
        well_weights[pl.ds(w * 8, 8), :] = strength
        picked = jnp.where(lane == y, strength, 0.0)
        for q in range(6):
            value = drawn[pl.ds(q * PLANE + x, 8, stride=XS), :] * picked
            total += pltpu.roll(value, (q * WELLS + w + LANES - y) & 127, 1)
    row = jnp.sum(total, axis=0, keepdims=True)
    message[pl.ds(22, CHUNKS, stride=MSG), :] = jnp.broadcast_to(row, (CHUNKS, LANES))
    message[pl.ds(23, CHUNKS, stride=MSG), :] = jnp.zeros((CHUNKS, LANES), F32)


def pick(matrix, chosen):
    high = matrix.astype(jnp.bfloat16)
    rest = matrix - high.astype(F32)
    middle = rest.astype(jnp.bfloat16)
    low = (rest - middle.astype(F32)).astype(jnp.bfloat16)
    chosen = chosen.astype(jnp.bfloat16)
    return (
        jnp.dot(high, chosen, preferred_element_type=F32)
        + jnp.dot(middle, chosen, preferred_element_type=F32)
        + jnp.dot(low, chosen, preferred_element_type=F32)
    )


def chain_kernel(ids, cells, message, reply, states):
    sub, lane = iota((8, LANES), 0), iota((8, LANES), 1)

    def spread(rows, first):
        pair = pltpu.roll(rows, (8 - first) % 8, 0) if first else rows
        pair = jnp.where(sub < 2, pair, 0.0)
        pair += pltpu.roll(pair, 2, 0)
        return pair + pltpu.roll(pair, 4, 0)

    tails = [message[pl.ds(l * MSG + 16, 8), :] for l in range(CHUNKS)]
    state = jnp.zeros((8, LANES), F32)
    entering = []
    for l in range(CHUNKS):
        entering.append(state)
        reply[pl.ds(l * MSG, 8), :] = state
        states[pl.ds(l * 8, 8), pl.ds(0, LANES)] = state
        if l < CHUNKS - 1:
            state = message[pl.ds(l * MSG, 8), :] + spread(tails[l], 0) * state
    state = jnp.zeros((8, LANES), F32)
    for l in reversed(range(CHUNKS)):
        reply[pl.ds(l * MSG + 8, 8), :] = state
        states[pl.ds(l * 8, 8), pl.ds(LANES, LANES)] = state
        if l > 0:
            state = (
                message[pl.ds(l * MSG + 8, 8), :]
                + spread(tails[l], 4) * entering[l]
                + spread(tails[l], 2) * state
            )
    me = ids[0, 0]
    wide = (2 * LANES, 2 * LANES)
    col = iota((1, 2 * LANES), 1)
    owner = jnp.zeros((1, 2 * LANES), jnp.int32)
    for w in range(WELLS):
        owner = jnp.where((col & 15) == w, cells[0, w], owner)
    line, column = iota(wide, 0), iota(wide, 1)
    place = (lax.shift_right_logical(column, 7) * 16 + me) * LANES + (line & 127)
    group = lax.shift_right_logical(column & 127, 4) - 4
    chosen = jnp.where(
        (jnp.broadcast_to(owner, wide) == place) & (group == lax.shift_right_logical(line, 7)),
        1.0,
        0.0,
    )
    found = pick(states[...], chosen)
    odd = (sub & 1) == 1
    total = jnp.zeros((8, LANES), F32)
    fixed = jnp.zeros((1, LANES), F32)
    for l in range(CHUNKS):
        row = tails[l][6:7, :]
        fixed += row
        here = found[l * 8 : l * 8 + 8, :]
        total += row * jnp.where(odd, here[:, LANES:], here[:, :LANES])
    rates = pltpu.roll(total, 64, 1) + pltpu.roll(total, 48, 1)
    fixed = jnp.broadcast_to(jnp.where(me == 0, fixed, 0.0), (8, LANES))
    for s in range(COLS):
        mine = fixed if s == 0 else pltpu.roll(fixed, LANES - 16 * s, 1)
        rates += jnp.where(sub == 2 * s, mine, 0.0)
    rates = jnp.where(lane < WELLS, rates, 0.0)
    for l in range(CHUNKS):
        reply[pl.ds(l * MSG + 16, 8), :] = rates


def precond_kernel(
    ids, send_rows, reply, base, from_below, from_above, krylov, diag0, diag3, diag6, inv,
    precond, x_a, x_b, layer_a, layer_b, outgoing, rates,
):
    for block in range(BLOCKS):
        below = [reply[chunk_rows(2 * s, block), :] for s in range(COLS)]
        above = [reply[chunk_rows(8 + 2 * s, block), :] for s in range(COLS)]
        for k in range(LAYERS):
            at = rows_at(0, k, block)
            low, high = from_below[at, :], from_above[at, :]
            diag = [diag0[at, :], diag3[at, :], diag6[at, :]]
            inverse = [inv[rows_at(e, k, block), :] for e in range(9)]
            for s in range(COLS):
                pressure = base[rows_at(s, k, block), :] + low * below[s] + high * above[s]
                residue = [
                    krylov[rows_at(s * 3 + c, k, block), :] - diag[c] * pressure
                    for c in range(COMPS)
                ]
                for c in range(COMPS):
                    value = (
                        inverse[3 * c] * residue[0]
                        + inverse[3 * c + 1] * residue[1]
                        + inverse[3 * c + 2] * residue[2]
                    )
                    precond[rows_at(s * 3 + c, k, block), :] = value + pressure if c == 0 else value
    layer_even = (ids[0, 0] & 1) == 0
    x_even = (ids[0, 1] & 1) == 0
    x_a[...] = precond[pl.ds(jnp.where(x_even, XS - 1, 0), 96, stride=XS), :]
    x_b[...] = precond[pl.ds(jnp.where(x_even, 0, XS - 1), 96, stride=XS), :]
    layer_first = pl.multiple_of(jnp.where(layer_even, (LAYERS - 1) * XS, 0), XS)
    layer_second = pl.multiple_of(jnp.where(layer_even, 0, (LAYERS - 1) * XS), XS)
    for plane in range(12):
        layer_a[pl.ds(plane * XS, XS), :] = precond[pl.ds(plane * PLANE + layer_first, XS), :]
        layer_b[pl.ds(plane * XS, XS), :] = precond[pl.ds(plane * PLANE + layer_second, XS), :]
    for u in range(TILES):
        for j in range(SLOTS):
            row = send_rows[j, u]
            outgoing[pl.ds(u * 96 + j * 8, 8), :] = precond[pl.ds(row, 8, stride=PLANE), :]
            outgoing[pl.ds(u * 96 + 64 + j * 4, 4), :] = precond[
                pl.ds(row + 8 * PLANE, 4, stride=PLANE), :
            ]
    total = reply[pl.ds(16, 8), :]
    for j in range(1, CHUNKS):
        total += reply[pl.ds(j * MSG + 16, 8), :]
    rates[...] = total


def image_kernel(
    ids, cells, recv_rows, counts, precond, across, x_a, x_b, layer_a, layer_b, arrived, coef,
    diag, faces, rates, well_weights, image, gram,
):
    sub, lane = iota((8, LANES), 0), iota((8, LANES), 1)
    layer_even = (ids[0, 0] & 1) == 0
    x_even = (ids[0, 1] & 1) == 0
    y_first = ids[0, 2] == 0
    image[...] = jnp.zeros(image.shape, F32)
    for u in range(TILES):
        for j in range(SLOTS):
            row = recv_rows[j, u]
            slot = u * SLOTS + j
            weight = jnp.where(j < counts[0, u], coef[pl.ds(slot, 1), :], 0.0)
            image[pl.ds(row, 8, stride=PLANE), :] -= weight * arrived[pl.ds(u * 96 + j * 8, 8), :]
            image[pl.ds(row + 8 * PLANE, 4, stride=PLANE), :] -= (
                weight * arrived[pl.ds(u * 96 + 64 + j * 4, 4), :]
            )
    rate = rates[...]
    rate = (rate + pltpu.roll(rate, 7, 0)) * (1.0 / PERFS)
    for w in range(WELLS):
        cell = cells[0, w]
        x, y = lax.shift_right_logical(cell, 7), cell & 127
        strength = well_weights[pl.ds(w * 8, 8), :]
        placed = pltpu.roll(jnp.where(lane == w, rate, 0.0), (y + LANES - w) & 127, 1)
        for s in range(COLS):
            image[pl.ds(s * 3 * PLANE + x, 8, stride=XS), :] += strength * placed[2 * s : 2 * s + 1, :]
    sums = {}
    row_x = iota((XS, LANES), 0)
    lane_y = iota((XS, LANES), 1)

    def column(k, _):
        def at(plane, size=XS, layer=None):
            layer = k if layer is None else layer
            return pl.ds(pl.multiple_of(plane * PLANE + layer * XS, XS), size)

        totals = list(_)
        blocks = [diag[at(e), :] for e in range(9)]
        face = [faces[at(f), :] for f in range(6)]
        images = []
        for s in range(COLS):
            value = [precond[at(s * 3 + c), :] for c in range(COMPS)]
            for c in range(COMPS):
                plane = s * 3 + c
                here = value[c]
                out = image[at(plane), :]
                out += blocks[3 * c] * value[0]
                out += blocks[3 * c + 1] * value[1]
                out += blocks[3 * c + 2] * value[2]
                edge = pl.ds(plane * XS, XS)
                inner = precond[at(plane, layer=jnp.maximum(k - 1, 0)), :]
                outer = jnp.where(layer_even, layer_b[edge, :], layer_a[edge, :])
                out -= face[0] * jnp.where(k == 0, outer, inner)
                inner = precond[at(plane, layer=jnp.minimum(k + 1, LAYERS - 1)), :]
                outer = jnp.where(layer_even, layer_a[edge, :], layer_b[edge, :])
                out -= face[1] * jnp.where(k == LAYERS - 1, outer, inner)
                side = pl.ds(plane * LAYERS + k, 1)
                first, second = x_a[side, :], x_b[side, :]
                outer = jnp.where(x_even, second, first)
                out -= face[2] * jnp.where(row_x == 0, outer, pltpu.roll(here, 1, 0))
                outer = jnp.where(x_even, first, second)
                out -= face[3] * jnp.where(row_x == XS - 1, outer, pltpu.roll(here, XS - 1, 0))
                other = across[at(plane), :]
                edge_low = jnp.where(y_first, 0.0, other)
                edge_high = jnp.where(y_first, other, 0.0)
                out -= face[4] * pltpu.roll(jnp.where(lane_y == LANES - 1, edge_low, here), 1, 1)
                out -= face[5] * pltpu.roll(jnp.where(lane_y == 0, edge_high, here), LANES - 1, 1)
                image[at(plane), :] = out
                images.append(out)
        n = 0
        for s in range(COLS):
            for t in range(s + 1):
                value = images[s * 3] * images[t * 3]
                value += images[s * 3 + 1] * images[t * 3 + 1]
                value += images[s * 3 + 2] * images[t * 3 + 2]
                totals[n] += jnp.sum(value.reshape(BLOCKS, 8, LANES), axis=0)
                n += 1
        return tuple(totals)

    sums = lax.fori_loop(
        0, LAYERS, column, tuple(jnp.zeros((8, LANES), F32) for _ in range(10))
    )
    packed = jnp.zeros((1, LANES), F32)
    lanes = iota((1, LANES), 1)
    for n in range(10):
        value = jnp.sum(jnp.sum(sums[n], axis=0, keepdims=True), axis=1, keepdims=True)
        packed = jnp.where(lanes == n, value, packed)
    gram[...] = jnp.broadcast_to(packed, gram.shape)


def factor_kernel(scale, gathered, image, q, factor):
    total = jnp.sum(gathered[...].reshape(-1, 8, LANES), axis=0)
    total = jnp.sum(total, axis=0, keepdims=True) * scale
    lanes = iota((1, LANES), 1)
    entry, n = {}, 0
    for s in range(COLS):
        for t in range(s + 1):
            entry[s, t] = jnp.sum(jnp.where(lanes == n, total, 0.0), axis=1, keepdims=True)
            n += 1
    lower = {}
    for t in range(COLS):
        value = entry[t, t]
        for i in range(t):
            value -= lower[t, i] * lower[t, i]
        lower[t, t] = jnp.sqrt(value)
        for s in range(t + 1, COLS):
            value = entry[s, t]
            for i in range(t):
                value -= lower[s, i] * lower[t, i]
            lower[s, t] = value / lower[t, t]
    line, col = iota((COLS, COLS), 0), iota((COLS, COLS), 1)
    result = jnp.zeros((COLS, COLS), F32)
    for (s, t), value in lower.items():
        result = jnp.where((line == t) & (col == s), value, result)
    factor[...] = result
    wide = {key: jnp.broadcast_to(value, (8, LANES)) for key, value in lower.items()}
    inverse = {t: 1.0 / wide[t, t] for t in range(COLS)}

    def step(i, _):
        at = pl.multiple_of(i * 8, 8)
        done = []
        for s in range(COLS):
            for_s = []
            for c in range(COMPS):
                value = image[pl.ds((s * 3 + c) * PLANE + at, 8), :]
                for t in range(s):
                    value -= wide[s, t] * done[t][c]
                value *= inverse[s]
                q[pl.ds((s * 3 + c) * PLANE + at, 8), :] = value
                for_s.append(value)
            done.append(for_s)
        return _

    lax.fori_loop(0, PLANE // 8, step, 0, unroll=4)


SMEM = pl.BlockSpec(memory_space=pltpu.SMEM)
VMEM = pl.BlockSpec(memory_space=pltpu.VMEM)


def part(plane, planes=1):
    return pl.BlockSpec((planes * PLANE, LANES), lambda i: (plane, 0))


def whole(rows):
    return pl.BlockSpec((rows, LANES), lambda i: (0, 0))


def shape(*rows):
    return tuple(jax.ShapeDtypeStruct((r, LANES), F32) for r in rows)


def call(kernel, name, outs, ins, smems=1, scratch=(), flops=1_000_000):
    def run(*args):
        specs = [SMEM] * smems
        for arg, spec in zip(args[smems:], ins, strict=True):
            specs.append(whole(arg.shape[0]) if spec is None else spec)
        size = sum(a.size * 4 for a in args)
        return pl.pallas_call(
            kernel,
            name=name,
            grid=(1,),
            out_shape=outs,
            in_specs=specs,
            out_specs=tuple(
                pl.BlockSpec(o.shape, lambda i: (0,) * len(o.shape)) for o in outs
            ),
            scratch_shapes=list(scratch),
            compiler_params=pltpu.CompilerParams(vmem_limit_bytes=60 << 20),
            cost_estimate=pl.CostEstimate(flops=flops, bytes_accessed=size, transcendentals=0),
        )(*args)

    return run


def pairs(size, odd):
    found = []
    for i in range(1 if odd else 0, size - 1, 2):
        found += [(i, i + 1), (i + 1, i)]
    return found


def on_device(
    krylov_block,
    weights,
    pivots,
    lower_ratio,
    upper_ratio,
    block_diag,
    block_inv,
    face_coef,
    fault_send_rows,
    fault_recv_rows,
    fault_counts,
    fault_coef,
    well_cells,
    well_perfs,
    well_index,
):
    n_layer, n_tx, n_ty = (lax.axis_size(a) for a in ALL)

    def flat(array):
        return array.reshape(-1, LANES)

    krylov, diag, inv, faces = (
        flat(a) for a in (krylov_block, block_diag, block_inv, face_coef)
    )
    ids = jnp.stack([lax.axis_index(a) for a in ALL]).astype(jnp.int32).reshape(1, 3)
    cells = well_cells.reshape(1, WELLS)
    perfs = well_perfs.reshape(WELLS, PERFS).T
    index = well_index.reshape(WELLS, PERFS).T
    send_rows = fault_send_rows.reshape(TILES, SLOTS).T
    recv_rows = fault_recv_rows.reshape(TILES, SLOTS).T
    counts = fault_counts.reshape(1, TILES)
    columns = (part(0), part(3), part(6))
    message, base, from_below, from_above, well_weights = call(
        sweep_kernel,
        "sweep",
        shape(CHUNKS * MSG, COLS * PLANE, PLANE, PLANE, WELLS * 8),
        (None,) * 5 + columns + (part(0, 3),),
        smems=4,
        scratch=(pltpu.VMEM((6 * PLANE, LANES), F32),),
    )(
        ids, cells, perfs, index, krylov, flat(weights), flat(pivots), flat(lower_ratio),
        flat(upper_ratio), diag, diag, diag, inv,
    )
    message = lax.all_to_all(
        message.reshape(CHUNKS, MSG, LANES), "layer", split_axis=0, concat_axis=0, tiled=True
    )
    (reply,) = call(
        chain_kernel,
        "chain",
        shape(CHUNKS * MSG),
        (None,),
        smems=2,
        scratch=(pltpu.VMEM((LANES, 2 * LANES), F32),),
    )(ids, cells, flat(message))
    reply = lax.all_to_all(
        reply.reshape(CHUNKS, MSG, LANES), "layer", split_axis=0, concat_axis=0, tiled=True
    )
    precond, x_a, x_b, layer_a, layer_b, outgoing, rates = call(
        precond_kernel,
        "precond",
        shape(12 * PLANE, 96, 96, 12 * XS, 12 * XS, TILES * 96, 8),
        (None,) * 5 + columns + (None,),
        smems=2,
    )(
        ids, send_rows, flat(reply), base, from_below, from_above, krylov, diag, diag, diag, inv
    )
    across = lax.ppermute(precond, "ty", pairs(n_ty, False))
    x_a = lax.ppermute(x_a, "tx", pairs(n_tx, False))
    x_b = lax.ppermute(x_b, "tx", pairs(n_tx, True))
    layer_a = lax.ppermute(layer_a, "layer", pairs(n_layer, False))
    layer_b = lax.ppermute(layer_b, "layer", pairs(n_layer, True))
    arrived = lax.all_to_all(
        outgoing.reshape(TILES, 96, LANES), ("tx", "ty"), split_axis=0, concat_axis=0, tiled=True
    )
    devices = n_layer * n_tx * n_ty
    image, gram = call(
        image_kernel,
        "image",
        shape(12 * PLANE, devices),
        (None,) * 12,
        smems=4,
    )(
        ids, cells, recv_rows, counts, precond, across, x_a, x_b, layer_a, layer_b, flat(arrived),
        flat(fault_coef), diag, faces, rates, well_weights,
    )
    gathered = lax.all_to_all(gram, ALL, split_axis=0, concat_axis=0, tiled=True)
    entries = float(12 * PLANE * LANES // COLS * devices)

    def factor(*refs):
        factor_kernel(1.0 / entries, *refs)

    q, r_factor = call(
        factor,
        "factor",
        shape(12 * PLANE) + (jax.ShapeDtypeStruct((COLS, COLS), F32),),
        (None, None),
        smems=0,
    )(gathered, image)
    return (q.reshape(krylov_block.shape), r_factor)


def solution(mesh):
    placed = (
        P(None, None, "layer", "tx", "ty"),
        P(None, "layer", "tx", "ty"),
        P("layer", "tx", "ty"),
        P("layer", "tx", "ty"),
        P("layer", "tx", "ty"),
        P(None, "layer", "tx", "ty"),
        P(None, "layer", "tx", "ty"),
        P(None, "layer", "tx", "ty"),
        P("layer", "tx", "ty", None, None),
        P("layer", "tx", "ty", None, None),
        P("layer", "tx", "ty", None),
        P("layer", "tx", "ty", None, None, None),
        P("tx", "ty", None),
        P("tx", "ty", None, None),
        P("tx", "ty", None, None),
    )
    return jax.shard_map(
        on_device,
        mesh=mesh,
        in_specs=placed,
        out_specs=(P(None, None, "layer", "tx", "ty"), P()),
        check_vma=False,
    )
```

```python
import jax
import jax.numpy as jnp
from jax import lax
from jax.experimental import pallas as pl
from jax.experimental.pallas import tpu as pltpu
from jax.sharding import PartitionSpec as P

F32 = jnp.float32
COLS, COMPS, LAYERS, XS, LANES = 4, 3, 8, 32, 128
BLOCKS = XS // 8
PLANE = LAYERS * XS
TILES, SLOTS = 16, 8
CHUNKS = 16
MSG = 24
WELLS, PERFS = 16, 8
ALL = ("layer", "tx", "ty")


def iota(shape, dim):
    return lax.broadcasted_iota(jnp.int32, shape, dim)


def rows_at(plane, layer, block):
    return pl.ds(plane * PLANE + layer * XS + block * 8, 8)


def chunk_rows(row, block):
    return pl.ds(MSG * 8 * (block % 2) + row + block // 2, 8, stride=MSG)


def fetch(copies, sems):
    handles = [
        pltpu.make_async_copy(a, b, sems.at[i]) for i, (a, b) in enumerate(copies)
    ]
    for handle in handles:
        handle.start()
    waited = []

    def ready(count=None):
        count = len(handles) if count is None else count
        while len(waited) < count:
            handles[len(waited)].wait()
            waited.append(None)

    return ready


def halves(pieces):
    return [
        (a.at[:, pl.ds(i * 16, 16)], b.at[:, pl.ds(i * 16, 16)]) for i in range(2) for a, b in pieces
    ]


def sweep_kernel(
    ids, cells_h, perfs_h, index_h, krylov_h, weights_h, pivots_h, lower_h, upper_h, diag_h, inv_h,
    message, base, from_below, from_above, well_weights,
    krylov, weights, pivots, lower, upper, diag, inv, cells, perfs, index, sems,
):
    pieces = [(krylov_h, krylov), (weights_h, weights), (pivots_h, pivots), (lower_h, lower)]
    pieces += [(upper_h, upper)]
    late = [(inv_h.at[pl.ds(0, 24)], inv)]
    late += [(diag_h.at[pl.ds(24 * c, 8)], diag.at[pl.ds(8 * c, 8)]) for c in range(3)]
    late += [(cells_h, cells), (perfs_h, perfs), (index_h, index)]
    ready = fetch(halves(pieces) + late, sems)
    for block in range(BLOCKS):
        half = block // 2 * len(pieces)
        xs = pl.ds(block * 8, 8)
        ready(half + 4)
        levels = [[] for _ in range(COLS)]
        products = []
        for k in range(LAYERS):
            restrict = [weights[c * 8 + k, xs, :] for c in range(COMPS)]
            pivot = pivots[k, xs, :]
            ratio = lower[k, xs, :]
            products.append(ratio if k == 0 else ratio * products[-1])
            for s in range(COLS):
                source = restrict[0] * krylov[s * 24 + k, xs, :]
                source += restrict[1] * krylov[s * 24 + 8 + k, xs, :]
                source += restrict[2] * krylov[s * 24 + 16 + k, xs, :]
                level = pivot * source
                levels[s].append(level if k == 0 else level + ratio * levels[s][-1])
        for s in range(COLS):
            message[chunk_rows(2 * s, block), :] = levels[s][-1]
        message[chunk_rows(16, block), :] = products[-1]
        ready(half + len(pieces))
        down = [None] * COLS
        low = high = None
        for k in reversed(range(LAYERS)):
            at = rows_at(0, k, block)
            ratio = upper[k, xs, :]
            first = k == LAYERS - 1
            low = products[k] if first else products[k] + ratio * low
            high = ratio if first else ratio * high
            from_below[at, :] = low
            from_above[at, :] = high
            for s in range(COLS):
                down[s] = levels[s][k] if first else levels[s][k] + ratio * down[s]
                base[rows_at(s, k, block), :] = down[s]
        for s in range(COLS):
            message[chunk_rows(8 + 2 * s, block), :] = down[s]
        message[chunk_rows(18, block), :] = high
        message[chunk_rows(20, block), :] = low
    ready()

    def near(ref, plane, x):
        return ref.reshape(-1, LANES)[pl.ds(plane * PLANE + x, 8, stride=XS), :]

    sub, lane = iota((8, LANES), 0), iota((8, LANES), 1)
    first_layer = ids[0, 0] * LAYERS
    total = jnp.zeros((8, LANES), F32)
    for w in range(WELLS):
        cell = cells[0, w]
        x, y = lax.shift_right_logical(cell, 7), cell & 127
        strength = jnp.zeros((8, LANES), F32)
        for p in range(PERFS):
            strength += jnp.where(sub == perfs[p, w] - first_layer, index[p, w], 0.0)
        well_weights[pl.ds(w * 8, 8), :] = strength
        picked = jnp.where(lane == y, strength, 0.0)
        column = [near(inv, c, x) for c in range(COMPS)]
        part = column[0] * near(diag, 0, x) + column[1] * near(diag, 1, x)
        part = picked * (1.0 - (part + column[2] * near(diag, 2, x)))
        values = []
        for s in range(COLS):
            value = column[0] * near(krylov, s * 3, x) + column[1] * near(krylov, s * 3 + 1, x)
            value += column[2] * near(krylov, s * 3 + 2, x)
            values.append(picked * value + part * base[pl.ds(s * PLANE + x, 8, stride=XS), :])
        values.append(part * from_below[pl.ds(x, 8, stride=XS), :])
        values.append(part * from_above[pl.ds(x, 8, stride=XS), :])
        for q in range(6):
            total += pltpu.roll(values[q], (q * WELLS + w + LANES - y) & 127, 1)
    row = jnp.sum(total, axis=0, keepdims=True)
    message[pl.ds(22, CHUNKS, stride=MSG), :] = jnp.broadcast_to(row, (CHUNKS, LANES))
    message[pl.ds(23, CHUNKS, stride=MSG), :] = jnp.zeros((CHUNKS, LANES), F32)


def split(matrix):
    high = matrix.astype(jnp.bfloat16)
    return high, (matrix - high.astype(F32)).astype(jnp.bfloat16)


def chain_kernel(ids, cells_h, message, reply, states, cells, sems):
    ready = fetch([(cells_h, cells)], sems)
    sub, lane = iota((8, LANES), 0), iota((8, LANES), 1)

    def spread(rows, first):
        pair = pltpu.roll(rows, (8 - first) % 8, 0) if first else rows
        pair = jnp.where(sub < 2, pair, 0.0)
        pair += pltpu.roll(pair, 2, 0)
        return pair + pltpu.roll(pair, 4, 0)

    tails = [message[pl.ds(l * MSG + 16, 8), :] for l in range(CHUNKS)]
    state = jnp.zeros((8, LANES), F32)
    entering = []
    for l in range(CHUNKS):
        entering.append(state)
        reply[pl.ds(l * MSG, 8), :] = state
        states[pl.ds(l * 8, 8), pl.ds(0, LANES)] = state
        if l < CHUNKS - 1:
            state = message[pl.ds(l * MSG, 8), :] + spread(tails[l], 0) * state
    state = jnp.zeros((8, LANES), F32)
    for l in reversed(range(CHUNKS)):
        reply[pl.ds(l * MSG + 8, 8), :] = state
        states[pl.ds(l * 8, 8), pl.ds(LANES, LANES)] = state
        if l > 0:
            state = (
                message[pl.ds(l * MSG + 8, 8), :]
                + spread(tails[l], 4) * entering[l]
                + spread(tails[l], 2) * state
            )
    ready()
    me = ids[0, 0]
    wide = (2 * LANES, 2 * LANES)
    col = iota((1, 2 * LANES), 1)
    owner = jnp.zeros((1, 2 * LANES), jnp.int32)
    for w in range(WELLS):
        owner = jnp.where((col & 15) == w, cells[0, w], owner)
    line, column = iota(wide, 0), iota(wide, 1)
    place = (lax.shift_right_logical(column, 7) * 16 + me) * LANES + (line & 127)
    group = lax.shift_right_logical(column & 127, 4) - 4
    chosen = jnp.where(
        (jnp.broadcast_to(owner, wide) == place) & (group == lax.shift_right_logical(line, 7)),
        1.0,
        0.0,
    )
    chosen = chosen.astype(jnp.bfloat16)
    found = sum(jnp.dot(p, chosen, preferred_element_type=F32) for p in split(states[...]))
    odd = (sub & 1) == 1
    total = jnp.zeros((8, LANES), F32)
    fixed = jnp.zeros((1, LANES), F32)
    for l in range(CHUNKS):
        row = tails[l][6:7, :]
        fixed += row
        here = found[l * 8 : l * 8 + 8, :]
        total += row * jnp.where(odd, here[:, LANES:], here[:, :LANES])
    rates = pltpu.roll(total, 64, 1) + pltpu.roll(total, 48, 1)
    fixed = jnp.broadcast_to(jnp.where(me == 0, fixed, 0.0), (8, LANES))
    for s in range(COLS):
        mine = fixed if s == 0 else pltpu.roll(fixed, LANES - 16 * s, 1)
        rates += jnp.where(sub == 2 * s, mine, 0.0)
    rates = jnp.where(lane < WELLS, rates, 0.0)
    for l in range(CHUNKS):
        reply[pl.ds(l * MSG + 16, 8), :] = rates


def ahead_kernel(
    krylov_h, diag_h, inv_h, base, from_below, from_above,
    fixed, by_below, by_above, krylov, diag, inv, sems,
):
    pieces = [(krylov_h, krylov), (inv_h, inv)]
    pieces += [(diag_h.at[pl.ds(24 * c, 8)], diag.at[pl.ds(8 * c, 8)]) for c in range(3)]
    ready = fetch(halves(pieces), sems)
    for block in range(BLOCKS):
        ready((block // 2 + 1) * len(pieces))
        xs = pl.ds(block * 8, 8)
        for k in range(LAYERS):
            at = rows_at(0, k, block)
            column = [diag[c * 8 + k, xs, :] for c in range(COMPS)]
            inverse = [inv[e * 8 + k, xs, :] for e in range(9)]
            low, high = from_below[at, :], from_above[at, :]
            share = []
            for c in range(COMPS):
                row = inverse[3 * c : 3 * c + 3]
                value = row[0] * column[0] + row[1] * column[1] + row[2] * column[2]
                share.append(1.0 - value if c == 0 else -value)
                by_below[rows_at(c, k, block), :] = share[c] * low
                by_above[rows_at(c, k, block), :] = share[c] * high
            for s in range(COLS):
                value = [krylov[(s * 3 + c) * 8 + k, xs, :] for c in range(COMPS)]
                pressure = base[rows_at(s, k, block), :]
                for c in range(COMPS):
                    row = inverse[3 * c : 3 * c + 3]
                    fixed[rows_at(s * 3 + c, k, block), :] = (
                        row[0] * value[0] + row[1] * value[1] + row[2] * value[2]
                    ) + share[c] * pressure


def precond_kernel(
    ids, send_rows_h, reply, fixed, by_below, by_above,
    precond, precond_h, x_a_h, x_b_h, layer_a_h, layer_b_h, outgoing_h, rates,
    x_a, x_b, outgoing, send_rows, sems,
):
    listed = fetch([(send_rows_h, send_rows)], sems.at[pl.ds(6, 1)])
    for block in range(BLOCKS):
        below = [reply[chunk_rows(2 * s, block), :] for s in range(COLS)]
        above = [reply[chunk_rows(8 + 2 * s, block), :] for s in range(COLS)]
        for k in range(LAYERS):
            for c in range(COMPS):
                at = rows_at(c, k, block)
                low, high = by_below[at, :], by_above[at, :]
                for s in range(COLS):
                    at = rows_at(s * 3 + c, k, block)
                    precond[at, :] = fixed[at, :] + low * below[s] + high * above[s]
    layer_even = (ids[0, 0] & 1) == 0
    x_even = (ids[0, 1] & 1) == 0
    layer_first = pl.multiple_of(jnp.where(layer_even, (LAYERS - 1) * XS, 0), XS)
    layer_second = pl.multiple_of(jnp.where(layer_even, 0, (LAYERS - 1) * XS), XS)
    planes = precond.reshape(12, PLANE, LANES)
    ready = fetch(
        [
            (precond, precond_h),
            (planes.at[:, pl.ds(layer_first, XS)], layer_a_h),
            (planes.at[:, pl.ds(layer_second, XS)], layer_b_h),
        ],
        sems,
    )
    x_a[...] = precond[pl.ds(jnp.where(x_even, XS - 1, 0), 96, stride=XS), :]
    x_b[...] = precond[pl.ds(jnp.where(x_even, 0, XS - 1), 96, stride=XS), :]
    listed()
    for u in range(TILES):
        for j in range(SLOTS):
            row = send_rows[j, u]
            outgoing[pl.ds(u * 96 + j, 8, stride=8), :] = precond[pl.ds(row, 8, stride=PLANE), :]
            outgoing[pl.ds(u * 96 + 64 + j, 4, stride=8), :] = precond[
                pl.ds(row + 8 * PLANE, 4, stride=PLANE), :
            ]
    sent = fetch(
        [(outgoing, outgoing_h), (x_a, x_a_h), (x_b, x_b_h)], sems.at[pl.ds(3, 3)]
    )
    total = reply[pl.ds(16, 8), :]
    for j in range(1, CHUNKS):
        total += reply[pl.ds(j * MSG + 16, 8), :]
    rates[...] = total
    ready()
    sent()


def stencil_kernel(
    ids, cells_h, recv_rows_h, counts_h, precond, across_h, layer_a_h, layer_b_h, diag_h, faces_h,
    rates, well_weights, image, edges, targets,
    across, layer_a, layer_b, diag, faces, cells, recv_rows, counts, sems,
):
    ready = fetch(
        [
            (cells_h, cells), (recv_rows_h, recv_rows), (counts_h, counts), (across_h, across),
            (layer_a_h, layer_a), (layer_b_h, layer_b), (diag_h, diag), (faces_h, faces),
        ],
        sems,
    )
    sub, lane = iota((8, LANES), 0), iota((8, LANES), 1)
    layer_even = (ids[0, 0] & 1) == 0
    y_first = ids[0, 2] == 0
    row_x = iota((XS, LANES), 0)
    lane_y = iota((XS, LANES), 1)
    ready()

    def column(k, _):
        def at(plane, layer=None):
            layer = k if layer is None else layer
            return pl.ds(pl.multiple_of(plane * PLANE + layer * XS, XS), XS)

        blocks = [diag[at(e), :] for e in range(9)]
        face = [faces[at(f), :] for f in range(6)]
        for s in range(COLS):
            value = [precond[at(s * 3 + c), :] for c in range(COMPS)]
            for c in range(COMPS):
                plane = s * 3 + c
                here = value[c]
                out = blocks[3 * c] * value[0]
                out += blocks[3 * c + 1] * value[1]
                out += blocks[3 * c + 2] * value[2]
                edge = pl.ds(plane * XS, XS)
                inner = precond[at(plane, jnp.maximum(k - 1, 0)), :]
                outer = jnp.where(layer_even, layer_b[edge, :], layer_a[edge, :])
                out -= face[0] * jnp.where(k == 0, outer, inner)
                inner = precond[at(plane, jnp.minimum(k + 1, LAYERS - 1)), :]
                outer = jnp.where(layer_even, layer_a[edge, :], layer_b[edge, :])
                out -= face[1] * jnp.where(k == LAYERS - 1, outer, inner)
                out -= face[2] * jnp.where(row_x == 0, 0.0, pltpu.roll(here, 1, 0))
                out -= face[3] * jnp.where(row_x == XS - 1, 0.0, pltpu.roll(here, XS - 1, 0))
                other = across[at(plane), :]
                edge_low = jnp.where(y_first, 0.0, other)
                edge_high = jnp.where(y_first, other, 0.0)
                out -= face[4] * pltpu.roll(jnp.where(lane_y == LANES - 1, edge_low, here), 1, 1)
                out -= face[5] * pltpu.roll(jnp.where(lane_y == 0, edge_high, here), LANES - 1, 1)
                image[at(plane), :] = out
        return _

    lax.fori_loop(0, LAYERS, column, 0)
    slot = iota((1, LANES), 1)
    target = jnp.full((1, LANES), -1, jnp.int32)
    for u in range(TILES):
        for j in range(SLOTS):
            row = jnp.where(j < counts[0, u], recv_rows[j, u], -1)
            target = jnp.where(slot == u * SLOTS + j, row, target)
    targets[...] = jnp.where(iota((PLANE, LANES), 0) == target, 1.0, 0.0)
    edges[pl.ds(0, 8), :] = faces[pl.ds(2 * PLANE, 8, stride=XS), :]
    edges[pl.ds(8, 8), :] = faces[pl.ds(3 * PLANE + XS - 1, 8, stride=XS), :]
    rate = rates[...]
    rate = (rate + pltpu.roll(rate, 7, 0)) * (1.0 / PERFS)
    for w in range(WELLS):
        cell = cells[0, w]
        x, y = lax.shift_right_logical(cell, 7), cell & 127
        strength = well_weights[pl.ds(w * 8, 8), :]
        placed = pltpu.roll(jnp.where(lane == w, rate, 0.0), (y + LANES - w) & 127, 1)
        for s in range(COLS):
            image[pl.ds(s * 3 * PLANE + x, 8, stride=XS), :] += strength * placed[2 * s : 2 * s + 1, :]


def finish_kernel(ids, _, x_a, x_b, arrived, coef_h, edges, targets, image, gram, coef, sems):
    ready = fetch([(coef_h, coef)], sems)
    x_even = (ids[0, 1] & 1) == 0
    for plane in range(12):
        side = pl.ds(plane * LAYERS, LAYERS)
        first, second = x_a[side, :], x_b[side, :]
        at = pl.ds(plane * PLANE, 8, stride=XS)
        image[at, :] -= edges[pl.ds(0, 8), :] * jnp.where(x_even, second, first)
        at = pl.ds(plane * PLANE + XS - 1, 8, stride=XS)
        image[at, :] -= edges[pl.ds(8, 8), :] * jnp.where(x_even, first, second)
    ready()
    chosen = targets[...].astype(jnp.bfloat16)
    chosen = jnp.concatenate([chosen, chosen], axis=1)
    weight = coef[...]
    for pair in range(6):
        parts = []
        for plane in (2 * pair, 2 * pair + 1):
            came = arrived[:, pl.ds(plane * 8, 8), :].reshape(TILES * SLOTS, LANES)
            parts.append(jnp.concatenate(split(came * weight), axis=0))
        added = jnp.dot(
            chosen, jnp.concatenate(parts, axis=1), preferred_element_type=F32
        )
        for i in range(2):
            at = pl.ds((2 * pair + i) * PLANE, PLANE)
            image[at, :] -= added[:, i * LANES : (i + 1) * LANES]

    def add(i, totals):
        at = pl.multiple_of(i * 8, 8)
        totals = list(totals)
        images = []
        for plane in range(12):
            value = image[pl.ds(plane * PLANE + at, 8), :]
            images.append(value)
        n = 0
        for s in range(COLS):
            for t in range(s + 1):
                value = images[s * 3] * images[t * 3]
                value += images[s * 3 + 1] * images[t * 3 + 1]
                value += images[s * 3 + 2] * images[t * 3 + 2]
                totals[n] += value
                n += 1
        return tuple(totals)

    sums = lax.fori_loop(
        0, PLANE // 8, add, tuple(jnp.zeros((8, LANES), F32) for _ in range(10)), unroll=4
    )
    packed = jnp.zeros((1, LANES), F32)
    lanes = iota((1, LANES), 1)
    for n in range(10):
        value = jnp.sum(jnp.sum(sums[n], axis=0, keepdims=True), axis=1, keepdims=True)
        packed = jnp.where(lanes == n, value, packed)
    gram[...] = jnp.broadcast_to(packed, gram.shape)


def factor_kernel(scale, gathered, image, q_h, factor_h, q, factor, sems):
    total = jnp.sum(gathered[...].reshape(-1, 8, LANES), axis=0)
    total = jnp.sum(total, axis=0, keepdims=True) * scale
    lanes = iota((1, LANES), 1)
    entry, n = {}, 0
    for s in range(COLS):
        for t in range(s + 1):
            entry[s, t] = jnp.sum(jnp.where(lanes == n, total, 0.0), axis=1, keepdims=True)
            n += 1
    lower = {}
    for t in range(COLS):
        value = entry[t, t]
        for i in range(t):
            value -= lower[t, i] * lower[t, i]
        lower[t, t] = jnp.sqrt(value)
        for s in range(t + 1, COLS):
            value = entry[s, t]
            for i in range(t):
                value -= lower[s, i] * lower[t, i]
            lower[s, t] = value / lower[t, t]
    line, col = iota((COLS, COLS), 0), iota((COLS, COLS), 1)
    result = jnp.zeros((COLS, COLS), F32)
    for (s, t), value in lower.items():
        result = jnp.where((line == t) & (col == s), value, result)
    factor[...] = result
    sent = [fetch([(factor, factor_h)], sems)]
    wide = {key: jnp.broadcast_to(value, (8, LANES)) for key, value in lower.items()}
    inverse = {t: 1.0 / wide[t, t] for t in range(COLS)}

    for half in range(4):

        def step(i, _, half=half):
            at = pl.multiple_of(half * 64 + i * 8, 8)
            done = []
            for s in range(COLS):
                for_s = []
                for c in range(COMPS):
                    value = image[pl.ds((s * 3 + c) * PLANE + at, 8), :]
                    for t in range(s):
                        value -= wide[s, t] * done[t][c]
                    value *= inverse[s]
                    q[s * 3 + c, pl.ds(at, 8), :] = value
                    for_s.append(value)
                done.append(for_s)
            return _

        lax.fori_loop(0, 8, step, 0, unroll=4)
        rows = pl.ds(half * 64, 64)
        sent.append(
            fetch([(q.at[:, rows], q_h.at[:, rows])], sems.at[pl.ds(1 + half, 1)])
        )
    for wait in sent:
        wait()


LIMIT = 24 << 20
SPACES = {"smem": pltpu.SMEM, "vmem": pltpu.VMEM, "hbm": pltpu.HBM}


def call(kernel, name, ins, outs, scratch=(), sems=1, flops=1_000_000, alias=None):
    args = [
        a if where == "smem" else pltpu.with_memory_space_constraint(a, SPACES[where])
        for a, where in ins
    ]
    size = sum(a.size * 4 for a in args)
    return pl.pallas_call(
        kernel,
        name=name,
        out_shape=tuple(SPACES[where](dims, F32) for dims, where in outs),
        in_specs=[pl.BlockSpec(memory_space=SPACES[where]) for _, where in ins],
        out_specs=tuple(pl.BlockSpec(memory_space=SPACES[where]) for _, where in outs),
        scratch_shapes=[pltpu.VMEM(d, F32) if isinstance(d, tuple) else d for d in scratch]
        + ([pltpu.SemaphoreType.DMA((sems,))] if sems else []),
        input_output_aliases=alias or {},
        compiler_params=pltpu.CompilerParams(vmem_limit_bytes=LIMIT),
        cost_estimate=pl.CostEstimate(flops=flops, bytes_accessed=size, transcendentals=0),
    )(*args)


def pairs(size, odd):
    found = []
    for i in range(1 if odd else 0, size - 1, 2):
        found += [(i, i + 1), (i + 1, i)]
    return found


def on_device(
    krylov_block,
    weights,
    pivots,
    lower_ratio,
    upper_ratio,
    block_diag,
    block_inv,
    face_coef,
    fault_send_rows,
    fault_recv_rows,
    fault_counts,
    fault_coef,
    well_cells,
    well_perfs,
    well_index,
):
    n_layer, n_tx, n_ty = (lax.axis_size(a) for a in ALL)

    def rows(array):
        return array.reshape(-1, LANES)

    def planes(array):
        return (array.reshape(-1, XS, LANES), "hbm")

    ids = jnp.stack([lax.axis_index(a) for a in ALL]).astype(jnp.int32).reshape(1, 3)
    ids = (ids, "smem")
    cells = (well_cells.reshape(1, WELLS), "hbm")
    perfs = (well_perfs.reshape(WELLS, PERFS).T, "hbm")
    index = (well_index.reshape(WELLS, PERFS).T, "hbm")
    send_rows = (fault_send_rows.reshape(TILES, SLOTS).T, "hbm")
    recv_rows = (fault_recv_rows.reshape(TILES, SLOTS).T, "hbm")
    counts = (fault_counts.reshape(1, TILES), "hbm")
    krylov, diag, inv = planes(krylov_block), planes(block_diag), planes(block_inv)
    fields = [planes(a) for a in (weights, pivots, lower_ratio, upper_ratio)]

    def line(count):
        return (count, LANES)

    message, base, from_below, from_above, well_weights = call(
        sweep_kernel,
        "sweep",
        [ids, cells, perfs, index, krylov, *fields, diag, inv],
        [
            (line(CHUNKS * MSG), "vmem"),
            (line(COLS * PLANE), "vmem"),
            (line(PLANE), "vmem"),
            (line(PLANE), "vmem"),
            (line(WELLS * 8), "vmem"),
        ],
        scratch=[(96, XS, LANES), (24, XS, LANES)]
        + [(8, XS, LANES)] * 3
        + [(24, XS, LANES)] * 2
        + [pltpu.SMEM((1, WELLS), jnp.int32), pltpu.SMEM((PERFS, WELLS), jnp.int32)]
        + [pltpu.SMEM((PERFS, WELLS), F32)],
        sems=17,
    )
    fixed, by_below, by_above = call(
        ahead_kernel,
        "ahead",
        [krylov, diag, inv, (base, "vmem"), (from_below, "vmem"), (from_above, "vmem")],
        [(line(12 * PLANE), "vmem"), (line(3 * PLANE), "vmem"), (line(3 * PLANE), "vmem")],
        scratch=[(96, XS, LANES), (24, XS, LANES), (72, XS, LANES)],
        sems=10,
    )
    message = lax.all_to_all(
        message.reshape(CHUNKS, MSG, LANES), "layer", split_axis=0, concat_axis=0, tiled=True
    )
    (reply,) = call(
        chain_kernel,
        "chain",
        [ids, cells, (rows(message), "vmem")],
        [(line(CHUNKS * MSG), "vmem")],
        scratch=[(LANES, 2 * LANES), pltpu.SMEM((1, WELLS), jnp.int32)],
        sems=1,
    )
    reply = lax.all_to_all(
        reply.reshape(CHUNKS, MSG, LANES), "layer", split_axis=0, concat_axis=0, tiled=True
    )
    precond, precond_out, x_a, x_b, layer_a, layer_b, outgoing, rates = call(
        precond_kernel,
        "precond",
        [
            ids, send_rows, (rows(reply), "vmem"), (fixed, "vmem"), (by_below, "vmem"),
            (by_above, "vmem"),
        ],
        [
            (line(12 * PLANE), "vmem"),
            (line(12 * PLANE), "hbm"),
            (line(96), "hbm"),
            (line(96), "hbm"),
            ((12, XS, LANES), "hbm"),
            ((12, XS, LANES), "hbm"),
            (line(TILES * 96), "hbm"),
            (line(8), "vmem"),
        ],
        scratch=[line(96), line(96), line(TILES * 96), pltpu.SMEM((SLOTS, TILES), jnp.int32)],
        sems=7,
    )
    across = lax.ppermute(precond_out, "ty", pairs(n_ty, False))
    x_a = lax.ppermute(x_a, "tx", pairs(n_tx, False))
    x_b = lax.ppermute(x_b, "tx", pairs(n_tx, True))
    layer_a = lax.ppermute(layer_a, "layer", pairs(n_layer, False))
    layer_b = lax.ppermute(layer_b, "layer", pairs(n_layer, True))
    arrived = lax.all_to_all(
        outgoing.reshape(TILES, 96, LANES), ("tx", "ty"), split_axis=0, concat_axis=0, tiled=True
    )
    devices = n_layer * n_tx * n_ty
    partial, edges, targets = call(
        stencil_kernel,
        "stencil",
        [
            ids, cells, recv_rows, counts, (precond, "vmem"), (across, "hbm"), (rows(layer_a), "hbm"),
            (rows(layer_b), "hbm"), (rows(block_diag), "hbm"), (rows(face_coef), "hbm"),
            (rates, "vmem"), (well_weights, "vmem"),
        ],
        [(line(12 * PLANE), "vmem"), (line(16), "vmem"), (line(PLANE), "vmem")],
        scratch=[line(12 * PLANE), line(12 * XS), line(12 * XS), line(9 * PLANE), line(6 * PLANE)]
        + [pltpu.SMEM((1, WELLS), jnp.int32), pltpu.SMEM((SLOTS, TILES), jnp.int32)]
        + [pltpu.SMEM((1, TILES), jnp.int32)],
        sems=8,
    )
    image, gram = call(
        finish_kernel,
        "finish",
        [
            ids, (partial, "vmem"), (x_a, "vmem"), (x_b, "vmem"), (arrived, "vmem"),
            (rows(fault_coef), "hbm"), (edges, "vmem"), (targets, "vmem"),
        ],
        [(line(12 * PLANE), "vmem"), (line(devices), "vmem")],
        scratch=[line(TILES * SLOTS)],
        alias={1: 0},
    )
    gathered = lax.all_to_all(gram, ALL, split_axis=0, concat_axis=0, tiled=True)
    entries = float(12 * PLANE * LANES // COLS * devices)

    def factor(*refs):
        factor_kernel(1.0 / entries, *refs)

    q, r_factor = call(
        factor,
        "factor",
        [(gathered, "vmem"), (image, "vmem")],
        [((12, PLANE, LANES), "hbm"), ((COLS, COLS), "hbm")],
        scratch=[(12, PLANE, LANES), (COLS, COLS)],
        sems=5,
    )
    return (q.reshape(krylov_block.shape), r_factor)


def solution(mesh):
    placed = (
        P(None, None, "layer", "tx", "ty"),
        P(None, "layer", "tx", "ty"),
        P("layer", "tx", "ty"),
        P("layer", "tx", "ty"),
        P("layer", "tx", "ty"),
        P(None, "layer", "tx", "ty"),
        P(None, "layer", "tx", "ty"),
        P(None, "layer", "tx", "ty"),
        P("layer", "tx", "ty", None, None),
        P("layer", "tx", "ty", None, None),
        P("layer", "tx", "ty", None),
        P("layer", "tx", "ty", None, None, None),
        P("tx", "ty", None),
        P("tx", "ty", None, None),
        P("tx", "ty", None, None),
    )
    return jax.shard_map(
        on_device,
        mesh=mesh,
        in_specs=placed,
        out_specs=(P(None, None, "layer", "tx", "ty"), P()),
        check_vma=False,
    )
```

```python
import jax
import jax.numpy as jnp
from jax import lax
from jax.experimental import pallas as pl
from jax.experimental.pallas import tpu as pltpu
from jax.sharding import PartitionSpec as P

F32 = jnp.float32
COLS, COMPS, LAYERS, XS, LANES = 4, 3, 8, 32, 128
BLOCKS = XS // 8
PLANE = LAYERS * XS
TILES, SLOTS = 16, 8
CHUNKS = 16
MSG = 24
WELLS, PERFS = 16, 8
ALL = ("layer", "tx", "ty")


def iota(shape, dim):
    return lax.broadcasted_iota(jnp.int32, shape, dim)


def rows_at(plane, layer, block):
    return pl.ds(plane * PLANE + layer * XS + block * 8, 8)


def chunk_rows(row, block):
    return pl.ds(MSG * 8 * (block % 2) + row + block // 2, 8, stride=MSG)


def fetch(copies, sems):
    handles = [
        pltpu.make_async_copy(a, b, sems.at[i]) for i, (a, b) in enumerate(copies)
    ]
    for handle in handles:
        handle.start()
    waited = []

    def ready(count=None):
        count = len(handles) if count is None else count
        while len(waited) < count:
            handles[len(waited)].wait()
            waited.append(None)

    return ready


def halves(pieces):
    return [
        (a.at[:, pl.ds(i * 16, 16)], b.at[:, pl.ds(i * 16, 16)]) for i in range(2) for a, b in pieces
    ]


def sweep_kernel(
    ids, cells_h, perfs_h, index_h, krylov_h, weights_h, pivots_h, lower_h, upper_h, diag_h, inv_h,
    message, base, from_below, from_above, strengths, owners,
    drawn, krylov, weights, pivots, lower, upper, diag, inv, cells, perfs, index, sems,
):
    pieces = [(krylov_h, krylov), (weights_h, weights), (pivots_h, pivots), (lower_h, lower)]
    pieces += [(upper_h, upper), (inv_h.at[pl.ds(0, 24)], inv)]
    pieces += [(diag_h.at[pl.ds(24 * c, 8)], diag.at[pl.ds(8 * c, 8)]) for c in range(3)]
    late = [(cells_h, cells), (perfs_h, perfs), (index_h, index)]
    ready = fetch(halves(pieces) + late, sems)
    for block in range(BLOCKS):
        half = block // 2 * len(pieces)
        xs = pl.ds(block * 8, 8)
        ready(half + 4)
        levels = [[] for _ in range(COLS)]
        products = []
        for k in range(LAYERS):
            restrict = [weights[c * 8 + k, xs, :] for c in range(COMPS)]
            pivot = pivots[k, xs, :]
            ratio = lower[k, xs, :]
            products.append(ratio if k == 0 else ratio * products[-1])
            for s in range(COLS):
                source = restrict[0] * krylov[s * 24 + k, xs, :]
                source += restrict[1] * krylov[s * 24 + 8 + k, xs, :]
                source += restrict[2] * krylov[s * 24 + 16 + k, xs, :]
                level = pivot * source
                levels[s].append(level if k == 0 else level + ratio * levels[s][-1])
        for s in range(COLS):
            message[chunk_rows(2 * s, block), :] = levels[s][-1]
        message[chunk_rows(16, block), :] = products[-1]
        ready(half + len(pieces))
        down = [None] * COLS
        low = high = None
        for k in reversed(range(LAYERS)):
            at = rows_at(0, k, block)
            ratio = upper[k, xs, :]
            first = k == LAYERS - 1
            low = products[k] if first else products[k] + ratio * low
            high = ratio if first else ratio * high
            from_below[at, :] = low
            from_above[at, :] = high
            inverse = [inv[c * 8 + k, xs, :] for c in range(COMPS)]
            share = 1.0 - (
                inverse[0] * diag[k, xs, :]
                + inverse[1] * diag[8 + k, xs, :]
                + inverse[2] * diag[16 + k, xs, :]
            )
            drawn[rows_at(4, k, block), :] = share * low
            drawn[rows_at(5, k, block), :] = share * high
            for s in range(COLS):
                down[s] = levels[s][k] if first else levels[s][k] + ratio * down[s]
                base[rows_at(s, k, block), :] = down[s]
                value = inverse[0] * krylov[s * 24 + k, xs, :]
                value += inverse[1] * krylov[s * 24 + 8 + k, xs, :]
                value += inverse[2] * krylov[s * 24 + 16 + k, xs, :]
                drawn[rows_at(s, k, block), :] = value + share * down[s]
        for s in range(COLS):
            message[chunk_rows(8 + 2 * s, block), :] = down[s]
        message[chunk_rows(18, block), :] = high
        message[chunk_rows(20, block), :] = low
    ready()
    sub, lane = iota((8, LANES), 0), iota((8, LANES), 1)
    layer = perfs[...] - ids[0, 0] * LAYERS
    strength = jnp.zeros((8, LANES), F32)
    for k in range(LAYERS):
        here = jnp.sum(jnp.where(layer == k, index[...], 0.0), axis=0, keepdims=True)
        here = jnp.concatenate([here, jnp.zeros((1, LANES - WELLS), F32)], axis=1)
        strength = jnp.where(sub == k, here, strength)
    strengths[...] = strength
    totals = [jnp.zeros((8, LANES), F32) for _ in range(6)]
    owner = jnp.zeros((8, LANES), jnp.int32)
    for w in range(WELLS):
        cell = cells[0, w]
        x, y = lax.shift_right_logical(cell, 7), cell & 127
        owner = jnp.where((lane & 15) == w, cell, owner)
        picked = pltpu.roll(jnp.where(lane == w, strength, 0.0), (y + LANES - w) & 127, 1)
        back = (w + LANES - y) & 127
        for q in range(6):
            value = drawn[pl.ds(q * PLANE + x, 8, stride=XS), :] * picked
            totals[q] += pltpu.roll(value, back, 1)
    owners[...] = owner - ids[0, 0] * LANES
    total = totals[0]
    for q in range(1, 6):
        total += pltpu.roll(totals[q], q * WELLS, 1)
    row = jnp.broadcast_to(jnp.sum(total, axis=0, keepdims=True), (CHUNKS, LANES))
    kept = (iota((CHUNKS, LANES), 0) == 0) | (iota((CHUNKS, LANES), 1) >= COLS * WELLS)
    message[pl.ds(22, CHUNKS, stride=MSG), :] = jnp.where(kept, row, 0.0)
    message[pl.ds(23, CHUNKS, stride=MSG), :] = jnp.zeros((CHUNKS, LANES), F32)


def split(matrix):
    high = matrix.astype(jnp.bfloat16)
    return high, (matrix - high.astype(F32)).astype(jnp.bfloat16)


def chain_kernel(owners, message, reply, states):
    sub, lane = iota((8, LANES), 0), iota((8, LANES), 1)

    def spread(rows, first):
        pair = pltpu.roll(rows, (8 - first) % 8, 0) if first else rows
        pair = jnp.where(sub < 2, pair, 0.0)
        pair += pltpu.roll(pair, 2, 0)
        return pair + pltpu.roll(pair, 4, 0)

    tails = [message[pl.ds(l * MSG + 16, 8), :] for l in range(CHUNKS)]
    state = jnp.zeros((8, LANES), F32)
    entering = []
    for l in range(CHUNKS):
        entering.append(state)
        reply[pl.ds(l * MSG, 8), :] = state
        states[pl.ds(l * 8, 8), pl.ds(0, LANES)] = state
        if l < CHUNKS - 1:
            state = message[pl.ds(l * MSG, 8), :] + spread(tails[l], 0) * state
    state = jnp.zeros((8, LANES), F32)
    for l in reversed(range(CHUNKS)):
        reply[pl.ds(l * MSG + 8, 8), :] = state
        states[pl.ds(l * 8, 8), pl.ds(LANES, LANES)] = state
        if l > 0:
            state = (
                message[pl.ds(l * MSG + 8, 8), :]
                + spread(tails[l], 4) * entering[l]
                + spread(tails[l], 2) * state
            )
    wide = (2 * LANES, 2 * LANES)
    owner = owners[0:1, :]
    owner = jnp.concatenate([owner, owner], axis=1)
    line, column = iota(wide, 0), iota(wide, 1)
    place = lax.shift_right_logical(column, 7) * (16 * LANES) + (line & 127)
    group = lax.shift_right_logical(column & 127, 4) - 4
    chosen = jnp.where(
        (jnp.broadcast_to(owner, wide) == place) & (group == lax.shift_right_logical(line, 7)),
        1.0,
        0.0,
    )
    chosen = chosen.astype(jnp.bfloat16)
    found = sum(jnp.dot(p, chosen, preferred_element_type=F32) for p in split(states[...]))
    odd = (sub & 1) == 1
    total = jnp.zeros((8, LANES), F32)
    fixed = jnp.zeros((1, LANES), F32)
    for l in range(CHUNKS):
        row = tails[l][6:7, :]
        fixed += row
        here = found[l * 8 : l * 8 + 8, :]
        total += row * jnp.where(odd, here[:, LANES:], here[:, :LANES])
    rates = pltpu.roll(total, 64, 1) + pltpu.roll(total, 48, 1)
    fixed = jnp.broadcast_to(fixed, (8, LANES))
    for s in range(COLS):
        mine = fixed if s == 0 else pltpu.roll(fixed, LANES - 16 * s, 1)
        rates += jnp.where(sub == 2 * s, mine, 0.0)
    rates = jnp.where(lane < WELLS, rates, 0.0)
    for l in range(CHUNKS):
        reply[pl.ds(l * MSG + 16, 8), :] = rates


def ahead_kernel(
    krylov_h, diag_h, inv_h, send_rows_h, base, from_below, from_above,
    fixed_h, by_below_h, by_above_h, fixed_rows, by_below_rows, by_above_rows, columns,
    fixed, by_below, by_above, krylov, diag, inv, send_rows, sems,
):
    pieces = [(krylov_h, krylov), (inv_h, inv)]
    pieces += [(diag_h.at[pl.ds(24 * c, 8)], diag.at[pl.ds(8 * c, 8)]) for c in range(3)]
    ready = fetch(halves(pieces) + [(send_rows_h, send_rows)], sems)
    for block in range(BLOCKS):
        ready((block // 2 + 1) * len(pieces))
        xs = pl.ds(block * 8, 8)
        for k in range(LAYERS):
            at = rows_at(0, k, block)
            column = [diag[c * 8 + k, xs, :] for c in range(COMPS)]
            inverse = [inv[e * 8 + k, xs, :] for e in range(9)]
            low, high = from_below[at, :], from_above[at, :]
            share = []
            for c in range(COMPS):
                row = inverse[3 * c : 3 * c + 3]
                value = row[0] * column[0] + row[1] * column[1] + row[2] * column[2]
                share.append(1.0 - value if c == 0 else -value)
                by_below[rows_at(c, k, block), :] = share[c] * low
                by_above[rows_at(c, k, block), :] = share[c] * high
            for s in range(COLS):
                value = [krylov[(s * 3 + c) * 8 + k, xs, :] for c in range(COMPS)]
                pressure = base[rows_at(s, k, block), :]
                for c in range(COMPS):
                    row = inverse[3 * c : 3 * c + 3]
                    fixed[rows_at(s * 3 + c, k, block), :] = (
                        row[0] * value[0] + row[1] * value[1] + row[2] * value[2]
                    ) + share[c] * pressure
    ready()
    sent = fetch(
        [(fixed, fixed_h), (by_below, by_below_h), (by_above, by_above_h)], sems.at[pl.ds(11, 3)]
    )
    col = iota((8, LANES), 1) & 31
    sub = iota((8, LANES), 0)
    for u in range(TILES):
        wanted = jnp.zeros((8, LANES), jnp.int32)
        for j in range(SLOTS):
            row = send_rows[j, u]
            wanted = jnp.where(sub == j, row & 31, wanted)
            fixed_rows[pl.ds(u * 96 + j, 8, stride=8), :] = fixed[pl.ds(row, 8, stride=PLANE), :]
            fixed_rows[pl.ds(u * 96 + 64 + j, 4, stride=8), :] = fixed[
                pl.ds(row + 8 * PLANE, 4, stride=PLANE), :
            ]
            at = pl.ds(u * 24 + j, 3, stride=8)
            by_below_rows[at, :] = by_below[pl.ds(row, 3, stride=PLANE), :]
            by_above_rows[at, :] = by_above[pl.ds(row, 3, stride=PLANE), :]
        columns[pl.ds(u * 8, 8), :] = jnp.where(col == wanted, 1.0, 0.0)
    sent()


def outgoing_kernel(reply, fixed_rows, by_below_rows, by_above_rows, columns, outgoing_h, outgoing, sems):
    planes = []
    for q in range(2 * COLS):
        planes.append(
            jnp.concatenate([reply[chunk_rows(2 * q, block), :] for block in range(BLOCKS)], axis=0)
        )
    states = jnp.concatenate(planes, axis=1)
    high = states.astype(jnp.bfloat16)
    rest = states - high.astype(F32)
    middle = rest.astype(jnp.bfloat16)
    low = (rest - middle.astype(F32)).astype(jnp.bfloat16)
    chosen = columns[:, 0:96].astype(jnp.bfloat16)
    stacked = jnp.concatenate([high, middle, low], axis=0)
    found = jnp.dot(chosen, stacked, preferred_element_type=F32)
    sent = []
    for u in range(TILES):
        here = found[u * 8 : u * 8 + 8, :]
        for c in range(COMPS):
            at = pl.ds(u * 24 + c * 8, 8)
            below, above = by_below_rows[at, :], by_above_rows[at, :]
            for s in range(COLS):
                at = pl.ds(u * 96 + (s * 3 + c) * 8, 8)
                outgoing[at, :] = (
                    fixed_rows[at, :]
                    + below * here[:, s * LANES : (s + 1) * LANES]
                    + above * here[:, (COLS + s) * LANES : (COLS + s + 1) * LANES]
                )
        if u % 8 == 7:
            at = pl.ds((u - 7) * 96, 8 * 96)
            copy = (outgoing.at[at], outgoing_h.at[at])
            sent.append(fetch([copy], sems.at[pl.ds(u // 8, 1)]))
    for wait in sent:
        wait()


def precond_kernel(
    ids, reply, fixed_h, by_below_h, by_above_h,
    precond_h, x_a_h, x_b_h, layer_a_h, layer_b_h, across_h, rates,
    precond, x_a, x_b, across, fixed, by_below, by_above, sems,
):
    ready = fetch(
        [(by_below_h, by_below), (by_above_h, by_above)]
        + [
            (fixed_h.at[pl.ds(s * 3 * PLANE, 3 * PLANE)], fixed.at[pl.ds(s * 3 * PLANE, 3 * PLANE)])
            for s in range(COLS)
        ],
        sems,
    )
    total = reply[pl.ds(16, 8), :]
    for j in range(1, CHUNKS):
        total += reply[pl.ds(j * MSG + 16, 8), :]
    rates[...] = total
    for s in range(COLS):
        ready(3 + s)
        for block in range(BLOCKS):
            below = reply[chunk_rows(2 * s, block), :]
            above = reply[chunk_rows(8 + 2 * s, block), :]
            for k in range(LAYERS):
                for c in range(COMPS):
                    at = rows_at(c, k, block)
                    low, high = by_below[at, :], by_above[at, :]
                    at = rows_at(s * 3 + c, k, block)
                    precond[at, :] = fixed[at, :] + low * below + high * above
    layer_even = (ids[0, 0] & 1) == 0
    x_even = (ids[0, 1] & 1) == 0
    layer_first = pl.multiple_of(jnp.where(layer_even, (LAYERS - 1) * XS, 0), XS)
    layer_second = pl.multiple_of(jnp.where(layer_even, 0, (LAYERS - 1) * XS), XS)
    planes = precond.reshape(12, PLANE, LANES)
    x_a[...] = precond[pl.ds(jnp.where(x_even, XS - 1, 0), 96, stride=XS), :]
    x_b[...] = precond[pl.ds(jnp.where(x_even, 0, XS - 1), 96, stride=XS), :]
    lane = iota((XS, LANES), 1)
    side = jnp.where(ids[0, 2] == 0, LANES - 1, 0)
    edge = jnp.zeros((XS, LANES), F32)
    for plane in range(96):
        value = pltpu.roll(precond[pl.ds(plane * XS, XS), :], (plane + LANES - side) & 127, 1)
        edge = jnp.where(lane == plane, value, edge)
    across[...] = edge
    sent = fetch(
        [
            (across, across_h),
            (x_a, x_a_h),
            (x_b, x_b_h),
            (planes.at[:, pl.ds(layer_first, XS)], layer_a_h),
            (planes.at[:, pl.ds(layer_second, XS)], layer_b_h),
            (precond, precond_h),
        ],
        sems.at[pl.ds(6, 6)],
    )
    sent()


def stencil_kernel(
    ids, cells_h, recv_rows_h, counts_h, precond_h, across_h, layer_a_h, layer_b_h, diag_h, faces_h,
    coef_h, rates, strengths, image, edges, targets, coef,
    precond, across, layer_a, layer_b, diag, faces, cells, recv_rows, counts, sems,
):
    ready = fetch(
        [
            (cells_h, cells), (recv_rows_h, recv_rows), (counts_h, counts), (precond_h, precond), (across_h, across),
            (layer_a_h, layer_a), (layer_b_h, layer_b), (diag_h, diag), (faces_h, faces),
            (coef_h, coef),
        ],
        sems,
    )
    sub, lane = iota((8, LANES), 0), iota((8, LANES), 1)
    layer_even = (ids[0, 0] & 1) == 0
    y_first = ids[0, 2] == 0
    side = jnp.where(y_first, LANES - 1, 0)
    row_x = iota((XS, LANES), 0)
    lane_y = iota((XS, LANES), 1)
    ready()

    def column(k, _):
        def at(plane, layer=None):
            layer = k if layer is None else layer
            return pl.ds(pl.multiple_of(plane * PLANE + layer * XS, XS), XS)

        blocks = [diag[at(e), :] for e in range(9)]
        face = [faces[at(f), :] for f in range(6)]
        for s in range(COLS):
            value = [precond[at(s * 3 + c), :] for c in range(COMPS)]
            for c in range(COMPS):
                plane = s * 3 + c
                here = value[c]
                out = blocks[3 * c] * value[0]
                out += blocks[3 * c + 1] * value[1]
                out += blocks[3 * c + 2] * value[2]
                edge = pl.ds(plane * XS, XS)
                inner = precond[at(plane, jnp.maximum(k - 1, 0)), :]
                outer = jnp.where(layer_even, layer_b[edge, :], layer_a[edge, :])
                out -= face[0] * jnp.where(k == 0, outer, inner)
                inner = precond[at(plane, jnp.minimum(k + 1, LAYERS - 1)), :]
                outer = jnp.where(layer_even, layer_a[edge, :], layer_b[edge, :])
                out -= face[1] * jnp.where(k == LAYERS - 1, outer, inner)
                out -= face[2] * jnp.where(row_x == 0, 0.0, pltpu.roll(here, 1, 0))
                out -= face[3] * jnp.where(row_x == XS - 1, 0.0, pltpu.roll(here, XS - 1, 0))
                other = pltpu.roll(across[...], (side + LANES - plane * LAYERS - k) & 127, 1)
                edge_low = jnp.where(y_first, 0.0, other)
                edge_high = jnp.where(y_first, other, 0.0)
                out -= face[4] * jnp.where(lane_y == 0, edge_low, pltpu.roll(here, 1, 1))
                out -= face[5] * jnp.where(
                    lane_y == LANES - 1, edge_high, pltpu.roll(here, LANES - 1, 1)
                )
                image[at(plane), :] = out
        return _

    lax.fori_loop(0, LAYERS, column, 0)
    slot = iota((1, LANES), 1)
    target = jnp.full((1, LANES), -1, jnp.int32)
    for u in range(TILES):
        for j in range(SLOTS):
            row = jnp.where(j < counts[0, u], recv_rows[j, u], -1)
            target = jnp.where(slot == u * SLOTS + j, row, target)
    targets[...] = jnp.where(iota((PLANE, LANES), 0) == target, 1.0, 0.0)
    edges[pl.ds(0, 8), :] = faces[pl.ds(2 * PLANE, 8, stride=XS), :]
    edges[pl.ds(8, 8), :] = faces[pl.ds(3 * PLANE + XS - 1, 8, stride=XS), :]
    rate = rates[...]
    rate = (rate + pltpu.roll(rate, 7, 0)) * (1.0 / PERFS)
    for w in range(WELLS):
        cell = cells[0, w]
        x, y = lax.shift_right_logical(cell, 7), cell & 127
        strength = jnp.broadcast_to(strengths[:, w : w + 1], (8, LANES))
        placed = pltpu.roll(jnp.where(lane == w, rate, 0.0), (y + LANES - w) & 127, 1)
        for s in range(COLS):
            image[pl.ds(s * 3 * PLANE + x, 8, stride=XS), :] += strength * placed[2 * s : 2 * s + 1, :]


def finish_kernel(ids, _, x_a, x_b, arrived, coef, edges, targets, image, gram):
    x_even = (ids[0, 1] & 1) == 0
    for plane in range(12):
        side = pl.ds(plane * LAYERS, LAYERS)
        first, second = x_a[side, :], x_b[side, :]
        at = pl.ds(plane * PLANE, 8, stride=XS)
        image[at, :] -= edges[pl.ds(0, 8), :] * jnp.where(x_even, second, first)
        at = pl.ds(plane * PLANE + XS - 1, 8, stride=XS)
        image[at, :] -= edges[pl.ds(8, 8), :] * jnp.where(x_even, first, second)
    chosen = targets[...].astype(jnp.bfloat16)
    chosen = jnp.concatenate([chosen, chosen], axis=1)
    weight = coef[...]
    for pair in range(6):
        parts = []
        for plane in (2 * pair, 2 * pair + 1):
            came = arrived[:, pl.ds(plane * 8, 8), :].reshape(TILES * SLOTS, LANES)
            parts.append(jnp.concatenate(split(came * weight), axis=0))
        added = jnp.dot(
            chosen, jnp.concatenate(parts, axis=1), preferred_element_type=F32
        )
        for i in range(2):
            at = pl.ds((2 * pair + i) * PLANE, PLANE)
            image[at, :] -= added[:, i * LANES : (i + 1) * LANES]

    def add(i, totals):
        at = pl.multiple_of(i * 8, 8)
        totals = list(totals)
        images = []
        for plane in range(12):
            value = image[pl.ds(plane * PLANE + at, 8), :]
            images.append(value)
        n = 0
        for s in range(COLS):
            for t in range(s + 1):
                value = images[s * 3] * images[t * 3]
                value += images[s * 3 + 1] * images[t * 3 + 1]
                value += images[s * 3 + 2] * images[t * 3 + 2]
                totals[n] += value
                n += 1
        return tuple(totals)

    sums = lax.fori_loop(
        0, PLANE // 8, add, tuple(jnp.zeros((8, LANES), F32) for _ in range(10)), unroll=4
    )
    packed = jnp.zeros((1, LANES), F32)
    lanes = iota((1, LANES), 1)
    for n in range(10):
        value = jnp.sum(jnp.sum(sums[n], axis=0, keepdims=True), axis=1, keepdims=True)
        packed = jnp.where(lanes == n, value, packed)
    gram[...] = jnp.broadcast_to(packed, gram.shape)


def factor_kernel(scale, gathered, image, q_h, factor_h, q, factor, sems):
    total = jnp.sum(gathered[...].reshape(-1, 8, LANES), axis=0)
    total = jnp.sum(total, axis=0, keepdims=True) * scale
    lanes = iota((1, LANES), 1)
    entry, n = {}, 0
    for s in range(COLS):
        for t in range(s + 1):
            entry[s, t] = jnp.sum(jnp.where(lanes == n, total, 0.0), axis=1, keepdims=True)
            n += 1
    lower = {}
    for t in range(COLS):
        value = entry[t, t]
        for i in range(t):
            value -= lower[t, i] * lower[t, i]
        lower[t, t] = jnp.sqrt(value)
        for s in range(t + 1, COLS):
            value = entry[s, t]
            for i in range(t):
                value -= lower[s, i] * lower[t, i]
            lower[s, t] = value / lower[t, t]
    line, col = iota((COLS, COLS), 0), iota((COLS, COLS), 1)
    result = jnp.zeros((COLS, COLS), F32)
    for (s, t), value in lower.items():
        result = jnp.where((line == t) & (col == s), value, result)
    factor[...] = result
    sent = [fetch([(factor, factor_h)], sems)]
    wide = {key: jnp.broadcast_to(value, (8, LANES)) for key, value in lower.items()}
    inverse = {t: 1.0 / wide[t, t] for t in range(COLS)}

    for half in range(4):

        def step(i, _, half=half):
            at = pl.multiple_of(half * 64 + i * 8, 8)
            done = []
            for s in range(COLS):
                for_s = []
                for c in range(COMPS):
                    value = image[pl.ds((s * 3 + c) * PLANE + at, 8), :]
                    for t in range(s):
                        value -= wide[s, t] * done[t][c]
                    value *= inverse[s]
                    q[s * 3 + c, pl.ds(at, 8), :] = value
                    for_s.append(value)
                done.append(for_s)
            return _

        lax.fori_loop(0, 8, step, 0, unroll=4)
        rows = pl.ds(half * 64, 64)
        sent.append(
            fetch([(q.at[:, rows], q_h.at[:, rows])], sems.at[pl.ds(1 + half, 1)])
        )
    for wait in sent:
        wait()


LIMIT = 24 << 20
SPACES = {"smem": pltpu.SMEM, "vmem": pltpu.VMEM, "hbm": pltpu.HBM}


def call(kernel, name, ins, outs, scratch=(), sems=1, flops=1_000_000, alias=None):
    args = [
        a if where == "smem" else pltpu.with_memory_space_constraint(a, SPACES[where])
        for a, where in ins
    ]
    size = sum(a.size * 4 for a in args)
    return pl.pallas_call(
        kernel,
        name=name,
        out_shape=tuple(SPACES[o[1]](o[0], o[2] if len(o) > 2 else F32) for o in outs),
        in_specs=[pl.BlockSpec(memory_space=SPACES[where]) for _, where in ins],
        out_specs=tuple(pl.BlockSpec(memory_space=SPACES[o[1]]) for o in outs),
        scratch_shapes=[pltpu.VMEM(d, F32) if isinstance(d, tuple) else d for d in scratch]
        + ([pltpu.SemaphoreType.DMA((sems,))] if sems else []),
        input_output_aliases=alias or {},
        compiler_params=pltpu.CompilerParams(vmem_limit_bytes=LIMIT),
        cost_estimate=pl.CostEstimate(flops=flops, bytes_accessed=size, transcendentals=0),
    )(*args)


def pairs(size, odd):
    found = []
    for i in range(1 if odd else 0, size - 1, 2):
        found += [(i, i + 1), (i + 1, i)]
    return found


def on_device(
    krylov_block,
    weights,
    pivots,
    lower_ratio,
    upper_ratio,
    block_diag,
    block_inv,
    face_coef,
    fault_send_rows,
    fault_recv_rows,
    fault_counts,
    fault_coef,
    well_cells,
    well_perfs,
    well_index,
):
    n_layer, n_tx, n_ty = (lax.axis_size(a) for a in ALL)

    def rows(array):
        return array.reshape(-1, LANES)

    def planes(array):
        return (array.reshape(-1, XS, LANES), "hbm")

    ids = jnp.stack([lax.axis_index(a) for a in ALL]).astype(jnp.int32).reshape(1, 3)
    ids = (ids, "smem")
    cells = (well_cells.reshape(1, WELLS), "hbm")
    perfs = (well_perfs.reshape(WELLS, PERFS).T, "hbm")
    index = (well_index.reshape(WELLS, PERFS).T, "hbm")
    send_rows = (fault_send_rows.reshape(TILES, SLOTS).T, "hbm")
    recv_rows = (fault_recv_rows.reshape(TILES, SLOTS).T, "hbm")
    counts = (fault_counts.reshape(1, TILES), "hbm")
    krylov, diag, inv = planes(krylov_block), planes(block_diag), planes(block_inv)
    fields = [planes(a) for a in (weights, pivots, lower_ratio, upper_ratio)]

    def line(count):
        return (count, LANES)

    message, base, from_below, from_above, strengths, owners = call(
        sweep_kernel,
        "sweep",
        [ids, cells, perfs, index, krylov, *fields, diag, inv],
        [
            (line(CHUNKS * MSG), "vmem"),
            (line(COLS * PLANE), "vmem"),
            (line(PLANE), "vmem"),
            (line(PLANE), "vmem"),
            (line(8), "vmem"),
            (line(8), "vmem", jnp.int32),
        ],
        scratch=[line(6 * PLANE), (96, XS, LANES), (24, XS, LANES)]
        + [(8, XS, LANES)] * 3
        + [(24, XS, LANES)] * 2
        + [pltpu.SMEM((1, WELLS), jnp.int32), pltpu.VMEM((PERFS, WELLS), jnp.int32)]
        + [(PERFS, WELLS)],
        sems=21,
    )
    fixed, by_below, by_above, fixed_rows, by_below_rows, by_above_rows, columns = call(
        ahead_kernel,
        "ahead",
        [krylov, diag, inv, send_rows, (base, "vmem"), (from_below, "vmem"), (from_above, "vmem")],
        [
            (line(12 * PLANE), "hbm"),
            (line(3 * PLANE), "hbm"),
            (line(3 * PLANE), "hbm"),
            (line(TILES * 96), "vmem"),
            (line(TILES * 24), "vmem"),
            (line(TILES * 24), "vmem"),
            (line(TILES * SLOTS), "vmem"),
        ],
        scratch=[line(12 * PLANE), line(3 * PLANE), line(3 * PLANE)]
        + [(96, XS, LANES), (24, XS, LANES), (72, XS, LANES)]
        + [pltpu.SMEM((SLOTS, TILES), jnp.int32)],
        sems=14,
    )
    message = lax.all_to_all(
        message.reshape(CHUNKS, MSG, LANES), "layer", split_axis=0, concat_axis=0, tiled=True
    )
    (reply,) = call(
        chain_kernel,
        "chain",
        [(owners, "vmem"), (rows(message), "vmem")],
        [(line(CHUNKS * MSG), "vmem")],
        scratch=[(LANES, 2 * LANES)],
        sems=0,
    )
    reply = lax.all_to_all(
        reply.reshape(CHUNKS, MSG, LANES), "layer", split_axis=0, concat_axis=0, tiled=True
    )
    reply = rows(reply)
    (outgoing,) = call(
        outgoing_kernel,
        "outgoing",
        [
            (reply, "vmem"), (fixed_rows, "vmem"), (by_below_rows, "vmem"),
            (by_above_rows, "vmem"), (columns, "vmem"),
        ],
        [(line(TILES * 96), "hbm")],
        scratch=[line(TILES * 96)],
        sems=2,
    )
    arrived = lax.all_to_all(
        outgoing.reshape(TILES, 96, LANES), ("tx", "ty"), split_axis=0, concat_axis=0, tiled=True
    )
    precond, x_a, x_b, layer_a, layer_b, across, rates = call(
        precond_kernel,
        "precond",
        [ids, (reply, "vmem"), (fixed, "hbm"), (by_below, "hbm"), (by_above, "hbm")],
        [
            (line(12 * PLANE), "hbm"),
            (line(96), "hbm"),
            (line(96), "hbm"),
            ((12, XS, LANES), "hbm"),
            ((12, XS, LANES), "hbm"),
            (line(XS), "hbm"),
            (line(8), "vmem"),
        ],
        scratch=[line(12 * PLANE), line(96), line(96), line(XS)]
        + [line(12 * PLANE), line(3 * PLANE), line(3 * PLANE)],
        sems=12,
    )
    across = lax.ppermute(across, "ty", pairs(n_ty, False))
    x_a = lax.ppermute(x_a, "tx", pairs(n_tx, False))
    x_b = lax.ppermute(x_b, "tx", pairs(n_tx, True))
    layer_a = lax.ppermute(layer_a, "layer", pairs(n_layer, False))
    layer_b = lax.ppermute(layer_b, "layer", pairs(n_layer, True))
    devices = n_layer * n_tx * n_ty
    partial, edges, targets, coef = call(
        stencil_kernel,
        "stencil",
        [
            ids, cells, recv_rows, counts, (precond, "hbm"), (across, "hbm"), (rows(layer_a), "hbm"),
            (rows(layer_b), "hbm"), (rows(block_diag), "hbm"), (rows(face_coef), "hbm"),
            (rows(fault_coef), "hbm"), (rates, "vmem"), (strengths, "vmem"),
        ],
        [
            (line(12 * PLANE), "vmem"),
            (line(16), "vmem"),
            (line(PLANE), "vmem"),
            (line(TILES * SLOTS), "vmem"),
        ],
        scratch=[line(12 * PLANE), line(XS), line(12 * XS), line(12 * XS), line(9 * PLANE), line(6 * PLANE)]
        + [pltpu.SMEM((1, WELLS), jnp.int32), pltpu.SMEM((SLOTS, TILES), jnp.int32)]
        + [pltpu.SMEM((1, TILES), jnp.int32)],
        sems=10,
    )
    image, gram = call(
        finish_kernel,
        "finish",
        [
            ids, (partial, "vmem"), (x_a, "vmem"), (x_b, "vmem"), (arrived, "vmem"),
            (coef, "vmem"), (edges, "vmem"), (targets, "vmem"),
        ],
        [(line(12 * PLANE), "vmem"), (line(devices), "vmem")],
        sems=0,
        alias={1: 0},
    )
    gathered = lax.all_to_all(gram, ALL, split_axis=0, concat_axis=0, tiled=True)
    entries = float(12 * PLANE * LANES // COLS * devices)

    def factor(*refs):
        factor_kernel(1.0 / entries, *refs)

    q, r_factor = call(
        factor,
        "factor",
        [(gathered, "vmem"), (image, "vmem")],
        [((12, PLANE, LANES), "hbm"), ((COLS, COLS), "hbm")],
        scratch=[(12, PLANE, LANES), (COLS, COLS)],
        sems=5,
    )
    return (q.reshape(krylov_block.shape), r_factor)


def solution(mesh):
    placed = (
        P(None, None, "layer", "tx", "ty"),
        P(None, "layer", "tx", "ty"),
        P("layer", "tx", "ty"),
        P("layer", "tx", "ty"),
        P("layer", "tx", "ty"),
        P(None, "layer", "tx", "ty"),
        P(None, "layer", "tx", "ty"),
        P(None, "layer", "tx", "ty"),
        P("layer", "tx", "ty", None, None),
        P("layer", "tx", "ty", None, None),
        P("layer", "tx", "ty", None),
        P("layer", "tx", "ty", None, None, None),
        P("tx", "ty", None),
        P("tx", "ty", None, None),
        P("tx", "ty", None, None),
    )
    return jax.shard_map(
        on_device,
        mesh=mesh,
        in_specs=placed,
        out_specs=(P(None, None, "layer", "tx", "ty"), P()),
        check_vma=False,
    )
```

```python
import jax
import jax.numpy as jnp
from jax import lax
from jax.experimental import pallas as pl
from jax.experimental.pallas import tpu as pltpu
from jax.sharding import PartitionSpec as P

F32 = jnp.float32
COLS, COMPS, LAYERS, XS, LANES = 4, 3, 8, 32, 128
BLOCKS = XS // 8
PLANE = LAYERS * XS
TILES, SLOTS = 16, 8
CHUNKS = 16
MSG = 24
WELLS, PERFS = 16, 8
ALL = ("layer", "tx", "ty")


def iota(shape, dim):
    return lax.broadcasted_iota(jnp.int32, shape, dim)


def rows_at(plane, layer, block):
    return pl.ds(plane * PLANE + layer * XS + block * 8, 8)


def chunk_rows(row, block):
    return pl.ds(MSG * 8 * (block % 2) + row + block // 2, 8, stride=MSG)


def fetch(copies, sems):
    handles = [
        pltpu.make_async_copy(a, b, sems.at[i]) for i, (a, b) in enumerate(copies)
    ]
    for handle in handles:
        handle.start()
    waited = []

    def ready(count=None):
        count = len(handles) if count is None else count
        while len(waited) < count:
            handles[len(waited)].wait()
            waited.append(None)

    return ready


def halves(pieces):
    return [
        (a.at[:, pl.ds(i * 16, 16)], b.at[:, pl.ds(i * 16, 16)]) for i in range(2) for a, b in pieces
    ]


def sweep_kernel(
    ids, cells_h, perfs_h, index_h, krylov_h, weights_h, pivots_h, lower_h, upper_h, diag_h, inv_h,
    message, base, from_below, from_above, strengths, owners,
    drawn, krylov, weights, pivots, lower, upper, diag, inv, cells, perfs, index, sems,
):
    pieces = [(krylov_h, krylov), (weights_h, weights), (pivots_h, pivots), (lower_h, lower)]
    pieces += [(upper_h, upper), (inv_h.at[pl.ds(0, 24)], inv)]
    pieces += [(diag_h.at[pl.ds(24 * c, 8)], diag.at[pl.ds(8 * c, 8)]) for c in range(3)]
    late = [(cells_h, cells), (perfs_h, perfs), (index_h, index)]
    ready = fetch(halves(pieces) + late, sems)
    for block in range(BLOCKS):
        half = block // 2 * len(pieces)
        xs = pl.ds(block * 8, 8)
        ready(half + 4)
        levels = [[] for _ in range(COLS)]
        products = []
        for k in range(LAYERS):
            restrict = [weights[c * 8 + k, xs, :] for c in range(COMPS)]
            pivot = pivots[k, xs, :]
            ratio = lower[k, xs, :]
            products.append(ratio if k == 0 else ratio * products[-1])
            for s in range(COLS):
                source = restrict[0] * krylov[s * 24 + k, xs, :]
                source += restrict[1] * krylov[s * 24 + 8 + k, xs, :]
                source += restrict[2] * krylov[s * 24 + 16 + k, xs, :]
                level = pivot * source
                levels[s].append(level if k == 0 else level + ratio * levels[s][-1])
        for s in range(COLS):
            message[chunk_rows(2 * s, block), :] = levels[s][-1]
        message[chunk_rows(16, block), :] = products[-1]
        ready(half + len(pieces))
        down = [None] * COLS
        low = high = None
        for k in reversed(range(LAYERS)):
            at = rows_at(0, k, block)
            ratio = upper[k, xs, :]
            first = k == LAYERS - 1
            low = products[k] if first else products[k] + ratio * low
            high = ratio if first else ratio * high
            from_below[at, :] = low
            from_above[at, :] = high
            inverse = [inv[c * 8 + k, xs, :] for c in range(COMPS)]
            share = 1.0 - (
                inverse[0] * diag[k, xs, :]
                + inverse[1] * diag[8 + k, xs, :]
                + inverse[2] * diag[16 + k, xs, :]
            )
            drawn[rows_at(4, k, block), :] = share * low
            drawn[rows_at(5, k, block), :] = share * high
            for s in range(COLS):
                down[s] = levels[s][k] if first else levels[s][k] + ratio * down[s]
                base[rows_at(s, k, block), :] = down[s]
                value = inverse[0] * krylov[s * 24 + k, xs, :]
                value += inverse[1] * krylov[s * 24 + 8 + k, xs, :]
                value += inverse[2] * krylov[s * 24 + 16 + k, xs, :]
                drawn[rows_at(s, k, block), :] = value + share * down[s]
        for s in range(COLS):
            message[chunk_rows(8 + 2 * s, block), :] = down[s]
        message[chunk_rows(18, block), :] = high
        message[chunk_rows(20, block), :] = low
    ready()
    sub, lane = iota((8, LANES), 0), iota((8, LANES), 1)
    layer = perfs[...] - ids[0, 0] * LAYERS
    strength = jnp.zeros((8, LANES), F32)
    for k in range(LAYERS):
        here = jnp.sum(jnp.where(layer == k, index[...], 0.0), axis=0, keepdims=True)
        here = jnp.concatenate([here, jnp.zeros((1, LANES - WELLS), F32)], axis=1)
        strength = jnp.where(sub == k, here, strength)
    strengths[...] = strength
    totals = [jnp.zeros((8, LANES), F32) for _ in range(6)]
    owner = jnp.zeros((8, LANES), jnp.int32)
    for w in range(WELLS):
        cell = cells[0, w]
        x, y = lax.shift_right_logical(cell, 7), cell & 127
        owner = jnp.where((lane & 15) == w, cell, owner)
        picked = pltpu.roll(jnp.where(lane == w, strength, 0.0), (y + LANES - w) & 127, 1)
        back = (w + LANES - y) & 127
        for q in range(6):
            value = drawn[pl.ds(q * PLANE + x, 8, stride=XS), :] * picked
            totals[q] += pltpu.roll(value, back, 1)
    owners[...] = owner - ids[0, 0] * LANES
    total = totals[0]
    for q in range(1, 6):
        total += pltpu.roll(totals[q], q * WELLS, 1)
    row = jnp.broadcast_to(jnp.sum(total, axis=0, keepdims=True), (CHUNKS, LANES))
    kept = (iota((CHUNKS, LANES), 0) == 0) | (iota((CHUNKS, LANES), 1) >= COLS * WELLS)
    message[pl.ds(22, CHUNKS, stride=MSG), :] = jnp.where(kept, row, 0.0)
    message[pl.ds(23, CHUNKS, stride=MSG), :] = jnp.zeros((CHUNKS, LANES), F32)


def split(matrix):
    high = matrix.astype(jnp.bfloat16)
    return high, (matrix - high.astype(F32)).astype(jnp.bfloat16)


def chain_kernel(owners, message, reply, states):
    sub, lane = iota((8, LANES), 0), iota((8, LANES), 1)

    def spread(rows, first):
        pair = pltpu.roll(rows, (8 - first) % 8, 0) if first else rows
        pair = jnp.where(sub < 2, pair, 0.0)
        pair += pltpu.roll(pair, 2, 0)
        return pair + pltpu.roll(pair, 4, 0)

    tails = [message[pl.ds(l * MSG + 16, 8), :] for l in range(CHUNKS)]
    state = jnp.zeros((8, LANES), F32)
    entering = []
    for l in range(CHUNKS):
        entering.append(state)
        reply[pl.ds(l * MSG, 8), :] = state
        states[pl.ds(l * 8, 8), pl.ds(0, LANES)] = state
        if l < CHUNKS - 1:
            state = message[pl.ds(l * MSG, 8), :] + spread(tails[l], 0) * state
    state = jnp.zeros((8, LANES), F32)
    for l in reversed(range(CHUNKS)):
        reply[pl.ds(l * MSG + 8, 8), :] = state
        states[pl.ds(l * 8, 8), pl.ds(LANES, LANES)] = state
        if l > 0:
            state = (
                message[pl.ds(l * MSG + 8, 8), :]
                + spread(tails[l], 4) * entering[l]
                + spread(tails[l], 2) * state
            )
    wide = (2 * LANES, 2 * LANES)
    owner = owners[0:1, :]
    owner = jnp.concatenate([owner, owner], axis=1)
    line, column = iota(wide, 0), iota(wide, 1)
    place = lax.shift_right_logical(column, 7) * (16 * LANES) + (line & 127)
    group = lax.shift_right_logical(column & 127, 4) - 4
    chosen = jnp.where(
        (jnp.broadcast_to(owner, wide) == place) & (group == lax.shift_right_logical(line, 7)),
        1.0,
        0.0,
    )
    chosen = chosen.astype(jnp.bfloat16)
    found = sum(jnp.dot(p, chosen, preferred_element_type=F32) for p in split(states[...]))
    odd = (sub & 1) == 1
    total = jnp.zeros((8, LANES), F32)
    fixed = jnp.zeros((1, LANES), F32)
    for l in range(CHUNKS):
        row = tails[l][6:7, :]
        fixed += row
        here = found[l * 8 : l * 8 + 8, :]
        total += row * jnp.where(odd, here[:, LANES:], here[:, :LANES])
    rates = pltpu.roll(total, 64, 1) + pltpu.roll(total, 48, 1)
    fixed = jnp.broadcast_to(fixed, (8, LANES))
    for s in range(COLS):
        mine = fixed if s == 0 else pltpu.roll(fixed, LANES - 16 * s, 1)
        rates += jnp.where(sub == 2 * s, mine, 0.0)
    rates = jnp.where(lane < WELLS, rates, 0.0)
    for l in range(CHUNKS):
        reply[pl.ds(l * MSG + 16, 8), :] = rates


def ahead_kernel(
    krylov_h, diag_h, inv_h, send_rows_h, base, from_below, from_above,
    fixed_h, by_below_h, by_above_h, fixed_rows, by_below_rows, by_above_rows, columns,
    fixed, by_below, by_above, krylov, diag, inv, send_rows, sems,
):
    pieces = [(krylov_h, krylov), (inv_h, inv)]
    pieces += [(diag_h.at[pl.ds(24 * c, 8)], diag.at[pl.ds(8 * c, 8)]) for c in range(3)]
    ready = fetch(halves(pieces) + [(send_rows_h, send_rows)], sems)
    for block in range(BLOCKS):
        ready((block // 2 + 1) * len(pieces))
        xs = pl.ds(block * 8, 8)
        for k in range(LAYERS):
            at = rows_at(0, k, block)
            column = [diag[c * 8 + k, xs, :] for c in range(COMPS)]
            inverse = [inv[e * 8 + k, xs, :] for e in range(9)]
            low, high = from_below[at, :], from_above[at, :]
            share = []
            for c in range(COMPS):
                row = inverse[3 * c : 3 * c + 3]
                value = row[0] * column[0] + row[1] * column[1] + row[2] * column[2]
                share.append(1.0 - value if c == 0 else -value)
                by_below[rows_at(c, k, block), :] = share[c] * low
                by_above[rows_at(c, k, block), :] = share[c] * high
            for s in range(COLS):
                value = [krylov[(s * 3 + c) * 8 + k, xs, :] for c in range(COMPS)]
                pressure = base[rows_at(s, k, block), :]
                for c in range(COMPS):
                    row = inverse[3 * c : 3 * c + 3]
                    fixed[rows_at(s * 3 + c, k, block), :] = (
                        row[0] * value[0] + row[1] * value[1] + row[2] * value[2]
                    ) + share[c] * pressure
    ready()
    sent = fetch(
        [(fixed, fixed_h), (by_below, by_below_h), (by_above, by_above_h)], sems.at[pl.ds(11, 3)]
    )
    col = iota((8, LANES), 1) & 31
    sub = iota((8, LANES), 0)
    for u in range(TILES):
        wanted = jnp.zeros((8, LANES), jnp.int32)
        for j in range(SLOTS):
            row = send_rows[j, u]
            wanted = jnp.where(sub == j, row & 31, wanted)
            fixed_rows[pl.ds(u * 96 + j, 8, stride=8), :] = fixed[pl.ds(row, 8, stride=PLANE), :]
            fixed_rows[pl.ds(u * 96 + 64 + j, 4, stride=8), :] = fixed[
                pl.ds(row + 8 * PLANE, 4, stride=PLANE), :
            ]
            at = pl.ds(u * 24 + j, 3, stride=8)
            by_below_rows[at, :] = by_below[pl.ds(row, 3, stride=PLANE), :]
            by_above_rows[at, :] = by_above[pl.ds(row, 3, stride=PLANE), :]
        columns[pl.ds(u * 8, 8), :] = jnp.where(col == wanted, 1.0, 0.0)
    sent()


def outgoing_kernel(reply, fixed_rows, by_below_rows, by_above_rows, columns, outgoing_h, outgoing, sems):
    planes = []
    for q in range(2 * COLS):
        planes.append(
            jnp.concatenate([reply[chunk_rows(2 * q, block), :] for block in range(BLOCKS)], axis=0)
        )
    states = jnp.concatenate(planes, axis=1)
    high = states.astype(jnp.bfloat16)
    rest = states - high.astype(F32)
    middle = rest.astype(jnp.bfloat16)
    low = (rest - middle.astype(F32)).astype(jnp.bfloat16)
    chosen = columns[:, 0:96].astype(jnp.bfloat16)
    stacked = jnp.concatenate([high, middle, low], axis=0)
    found = jnp.dot(chosen, stacked, preferred_element_type=F32)
    sent = []
    for u in range(TILES):
        here = found[u * 8 : u * 8 + 8, :]
        for c in range(COMPS):
            at = pl.ds(u * 24 + c * 8, 8)
            below, above = by_below_rows[at, :], by_above_rows[at, :]
            for s in range(COLS):
                at = pl.ds(u * 96 + (s * 3 + c) * 8, 8)
                outgoing[at, :] = (
                    fixed_rows[at, :]
                    + below * here[:, s * LANES : (s + 1) * LANES]
                    + above * here[:, (COLS + s) * LANES : (COLS + s + 1) * LANES]
                )
        if u % 8 == 7:
            at = pl.ds((u - 7) * 96, 8 * 96)
            copy = (outgoing.at[at], outgoing_h.at[at])
            sent.append(fetch([copy], sems.at[pl.ds(u // 8, 1)]))
    for wait in sent:
        wait()


def precond_kernel(
    ids, reply, fixed_h, by_below_h, by_above_h,
    precond_h, x_a_h, x_b_h, layer_a_h, layer_b_h, across_h, rates,
    precond, x_a, x_b, across, fixed, by_below, by_above, sems,
):
    ready = fetch(
        [(by_below_h, by_below), (by_above_h, by_above)]
        + [
            (fixed_h.at[pl.ds(s * 3 * PLANE, 3 * PLANE)], fixed.at[pl.ds(s * 3 * PLANE, 3 * PLANE)])
            for s in range(COLS)
        ],
        sems,
    )
    total = reply[pl.ds(16, 8), :]
    for j in range(1, CHUNKS):
        total += reply[pl.ds(j * MSG + 16, 8), :]
    rates[...] = total
    written = []
    for s in range(COLS):
        ready(3 + s)
        for block in range(BLOCKS):
            below = reply[chunk_rows(2 * s, block), :]
            above = reply[chunk_rows(8 + 2 * s, block), :]
            for k in range(LAYERS):
                for c in range(COMPS):
                    at = rows_at(c, k, block)
                    low, high = by_below[at, :], by_above[at, :]
                    at = rows_at(s * 3 + c, k, block)
                    precond[at, :] = fixed[at, :] + low * below + high * above
        at = pl.ds(s * 3 * PLANE, 3 * PLANE)
        copy = (precond.at[at], precond_h.at[at])
        written.append(fetch([copy], sems.at[pl.ds(11 + s, 1)]))
    layer_even = (ids[0, 0] & 1) == 0
    x_even = (ids[0, 1] & 1) == 0
    layer_first = pl.multiple_of(jnp.where(layer_even, (LAYERS - 1) * XS, 0), XS)
    layer_second = pl.multiple_of(jnp.where(layer_even, 0, (LAYERS - 1) * XS), XS)
    planes = precond.reshape(12, PLANE, LANES)
    x_a[...] = precond[pl.ds(jnp.where(x_even, XS - 1, 0), 96, stride=XS), :]
    x_b[...] = precond[pl.ds(jnp.where(x_even, 0, XS - 1), 96, stride=XS), :]
    lane = iota((XS, LANES), 1)
    side = jnp.where(ids[0, 2] == 0, LANES - 1, 0)
    edge = jnp.zeros((XS, LANES), F32)
    for plane in range(96):
        value = pltpu.roll(precond[pl.ds(plane * XS, XS), :], (plane + LANES - side) & 127, 1)
        edge = jnp.where(lane == plane, value, edge)
    across[...] = edge
    sent = fetch(
        [
            (across, across_h),
            (x_a, x_a_h),
            (x_b, x_b_h),
            (planes.at[:, pl.ds(layer_first, XS)], layer_a_h),
            (planes.at[:, pl.ds(layer_second, XS)], layer_b_h),
        ],
        sems.at[pl.ds(6, 5)],
    )
    for wait in [sent] + written:
        wait()


def stencil_kernel(
    ids, cells_h, recv_rows_h, counts_h, precond_h, across_h, layer_a_h, layer_b_h, diag_h, faces_h,
    coef_h, rates, strengths, image, edges, targets, coef,
    precond, across, layer_a, layer_b, diag, faces, cells, recv_rows, counts, sems,
):
    ready = fetch(
        [
            (cells_h, cells), (recv_rows_h, recv_rows), (counts_h, counts), (precond_h, precond), (across_h, across),
            (layer_a_h, layer_a), (layer_b_h, layer_b), (diag_h, diag), (faces_h, faces),
            (coef_h, coef),
        ],
        sems,
    )
    sub, lane = iota((8, LANES), 0), iota((8, LANES), 1)
    layer_even = (ids[0, 0] & 1) == 0
    y_first = ids[0, 2] == 0
    side = jnp.where(y_first, LANES - 1, 0)
    row_x = iota((XS, LANES), 0)
    lane_y = iota((XS, LANES), 1)
    ready(3)
    slot = iota((1, LANES), 1)
    target = jnp.full((1, LANES), -1, jnp.int32)
    for u in range(TILES):
        for j in range(SLOTS):
            row = jnp.where(j < counts[0, u], recv_rows[j, u], -1)
            target = jnp.where(slot == u * SLOTS + j, row, target)
    targets[...] = jnp.where(iota((PLANE, LANES), 0) == target, 1.0, 0.0)
    ready()

    def column(k, _):
        def at(plane, layer=None):
            layer = k if layer is None else layer
            return pl.ds(pl.multiple_of(plane * PLANE + layer * XS, XS), XS)

        blocks = [diag[at(e), :] for e in range(9)]
        face = [faces[at(f), :] for f in range(6)]
        for s in range(COLS):
            value = [precond[at(s * 3 + c), :] for c in range(COMPS)]
            for c in range(COMPS):
                plane = s * 3 + c
                here = value[c]
                out = blocks[3 * c] * value[0]
                out += blocks[3 * c + 1] * value[1]
                out += blocks[3 * c + 2] * value[2]
                edge = pl.ds(plane * XS, XS)
                inner = precond[at(plane, jnp.maximum(k - 1, 0)), :]
                outer = jnp.where(layer_even, layer_b[edge, :], layer_a[edge, :])
                out -= face[0] * jnp.where(k == 0, outer, inner)
                inner = precond[at(plane, jnp.minimum(k + 1, LAYERS - 1)), :]
                outer = jnp.where(layer_even, layer_a[edge, :], layer_b[edge, :])
                out -= face[1] * jnp.where(k == LAYERS - 1, outer, inner)
                out -= face[2] * jnp.where(row_x == 0, 0.0, pltpu.roll(here, 1, 0))
                out -= face[3] * jnp.where(row_x == XS - 1, 0.0, pltpu.roll(here, XS - 1, 0))
                other = pltpu.roll(across[...], (side + LANES - plane * LAYERS - k) & 127, 1)
                edge_low = jnp.where(y_first, 0.0, other)
                edge_high = jnp.where(y_first, other, 0.0)
                out -= face[4] * jnp.where(lane_y == 0, edge_low, pltpu.roll(here, 1, 1))
                out -= face[5] * jnp.where(
                    lane_y == LANES - 1, edge_high, pltpu.roll(here, LANES - 1, 1)
                )
                image[at(plane), :] = out
        return _

    lax.fori_loop(0, LAYERS, column, 0)
    edges[pl.ds(0, 8), :] = faces[pl.ds(2 * PLANE, 8, stride=XS), :]
    edges[pl.ds(8, 8), :] = faces[pl.ds(3 * PLANE + XS - 1, 8, stride=XS), :]
    rate = rates[...]
    rate = (rate + pltpu.roll(rate, 7, 0)) * (1.0 / PERFS)
    for w in range(WELLS):
        cell = cells[0, w]
        x, y = lax.shift_right_logical(cell, 7), cell & 127
        strength = jnp.broadcast_to(strengths[:, w : w + 1], (8, LANES))
        placed = pltpu.roll(jnp.where(lane == w, rate, 0.0), (y + LANES - w) & 127, 1)
        for s in range(COLS):
            image[pl.ds(s * 3 * PLANE + x, 8, stride=XS), :] += strength * placed[2 * s : 2 * s + 1, :]


def finish_kernel(ids, _, x_a, x_b, arrived, coef, edges, targets, image, gram):
    x_even = (ids[0, 1] & 1) == 0
    for plane in range(12):
        side = pl.ds(plane * LAYERS, LAYERS)
        first, second = x_a[side, :], x_b[side, :]
        at = pl.ds(plane * PLANE, 8, stride=XS)
        image[at, :] -= edges[pl.ds(0, 8), :] * jnp.where(x_even, second, first)
        at = pl.ds(plane * PLANE + XS - 1, 8, stride=XS)
        image[at, :] -= edges[pl.ds(8, 8), :] * jnp.where(x_even, first, second)
    chosen = targets[...].astype(jnp.bfloat16)
    chosen = jnp.concatenate([chosen, chosen], axis=1)
    weight = coef[...]
    for pair in range(6):
        parts = []
        for plane in (2 * pair, 2 * pair + 1):
            came = arrived[:, pl.ds(plane * 8, 8), :].reshape(TILES * SLOTS, LANES)
            parts.append(jnp.concatenate(split(came * weight), axis=0))
        added = jnp.dot(
            chosen, jnp.concatenate(parts, axis=1), preferred_element_type=F32
        )
        for i in range(2):
            at = pl.ds((2 * pair + i) * PLANE, PLANE)
            image[at, :] -= added[:, i * LANES : (i + 1) * LANES]

    def add(i, totals):
        at = pl.multiple_of(i * 8, 8)
        totals = list(totals)
        images = []
        for plane in range(12):
            value = image[pl.ds(plane * PLANE + at, 8), :]
            images.append(value)
        n = 0
        for s in range(COLS):
            for t in range(s + 1):
                value = images[s * 3] * images[t * 3]
                value += images[s * 3 + 1] * images[t * 3 + 1]
                value += images[s * 3 + 2] * images[t * 3 + 2]
                totals[n] += value
                n += 1
        return tuple(totals)

    sums = lax.fori_loop(
        0, PLANE // 8, add, tuple(jnp.zeros((8, LANES), F32) for _ in range(10)), unroll=4
    )
    packed = jnp.zeros((1, LANES), F32)
    lanes = iota((1, LANES), 1)
    for n in range(10):
        value = jnp.sum(jnp.sum(sums[n], axis=0, keepdims=True), axis=1, keepdims=True)
        packed = jnp.where(lanes == n, value, packed)
    gram[...] = jnp.broadcast_to(packed, gram.shape)


def factor_kernel(scale, gathered, image, q_h, factor_h, q, factor, sems):
    total = jnp.sum(gathered[...].reshape(-1, 8, LANES), axis=0)
    total = jnp.sum(total, axis=0, keepdims=True) * scale
    lanes = iota((1, LANES), 1)
    entry, n = {}, 0
    for s in range(COLS):
        for t in range(s + 1):
            entry[s, t] = jnp.sum(jnp.where(lanes == n, total, 0.0), axis=1, keepdims=True)
            n += 1
    lower = {}
    for t in range(COLS):
        value = entry[t, t]
        for i in range(t):
            value -= lower[t, i] * lower[t, i]
        lower[t, t] = jnp.sqrt(value)
        for s in range(t + 1, COLS):
            value = entry[s, t]
            for i in range(t):
                value -= lower[s, i] * lower[t, i]
            lower[s, t] = value / lower[t, t]
    line, col = iota((COLS, COLS), 0), iota((COLS, COLS), 1)
    result = jnp.zeros((COLS, COLS), F32)
    for (s, t), value in lower.items():
        result = jnp.where((line == t) & (col == s), value, result)
    factor[...] = result
    sent = [fetch([(factor, factor_h)], sems)]
    wide = {key: jnp.broadcast_to(value, (8, LANES)) for key, value in lower.items()}
    inverse = {t: 1.0 / wide[t, t] for t in range(COLS)}

    for half in range(4):

        def step(i, _, half=half):
            at = pl.multiple_of(half * 64 + i * 8, 8)
            done = []
            for s in range(COLS):
                for_s = []
                for c in range(COMPS):
                    value = image[pl.ds((s * 3 + c) * PLANE + at, 8), :]
                    for t in range(s):
                        value -= wide[s, t] * done[t][c]
                    value *= inverse[s]
                    q[s * 3 + c, pl.ds(at, 8), :] = value
                    for_s.append(value)
                done.append(for_s)
            return _

        lax.fori_loop(0, 8, step, 0, unroll=4)
        rows = pl.ds(half * 64, 64)
        sent.append(
            fetch([(q.at[:, rows], q_h.at[:, rows])], sems.at[pl.ds(1 + half, 1)])
        )
    for wait in sent:
        wait()


LIMIT = 24 << 20
SPACES = {"smem": pltpu.SMEM, "vmem": pltpu.VMEM, "hbm": pltpu.HBM}


def call(kernel, name, ins, outs, scratch=(), sems=1, flops=1_000_000, alias=None):
    args = [
        a if where == "smem" else pltpu.with_memory_space_constraint(a, SPACES[where])
        for a, where in ins
    ]
    size = sum(a.size * 4 for a in args)
    return pl.pallas_call(
        kernel,
        name=name,
        out_shape=tuple(SPACES[o[1]](o[0], o[2] if len(o) > 2 else F32) for o in outs),
        in_specs=[pl.BlockSpec(memory_space=SPACES[where]) for _, where in ins],
        out_specs=tuple(pl.BlockSpec(memory_space=SPACES[o[1]]) for o in outs),
        scratch_shapes=[pltpu.VMEM(d, F32) if isinstance(d, tuple) else d for d in scratch]
        + ([pltpu.SemaphoreType.DMA((sems,))] if sems else []),
        input_output_aliases=alias or {},
        compiler_params=pltpu.CompilerParams(vmem_limit_bytes=LIMIT),
        cost_estimate=pl.CostEstimate(flops=flops, bytes_accessed=size, transcendentals=0),
    )(*args)


def pairs(size, odd):
    found = []
    for i in range(1 if odd else 0, size - 1, 2):
        found += [(i, i + 1), (i + 1, i)]
    return found


def on_device(
    krylov_block,
    weights,
    pivots,
    lower_ratio,
    upper_ratio,
    block_diag,
    block_inv,
    face_coef,
    fault_send_rows,
    fault_recv_rows,
    fault_counts,
    fault_coef,
    well_cells,
    well_perfs,
    well_index,
):
    n_layer, n_tx, n_ty = (lax.axis_size(a) for a in ALL)

    def rows(array):
        return array.reshape(-1, LANES)

    def planes(array):
        return (array.reshape(-1, XS, LANES), "hbm")

    ids = jnp.stack([lax.axis_index(a) for a in ALL]).astype(jnp.int32).reshape(1, 3)
    ids = (ids, "smem")
    cells = (well_cells.reshape(1, WELLS), "hbm")
    perfs = (well_perfs.reshape(WELLS, PERFS).T, "hbm")
    index = (well_index.reshape(WELLS, PERFS).T, "hbm")
    send_rows = (fault_send_rows.reshape(TILES, SLOTS).T, "hbm")
    recv_rows = (fault_recv_rows.reshape(TILES, SLOTS).T, "hbm")
    counts = (fault_counts.reshape(1, TILES), "hbm")
    krylov, diag, inv = planes(krylov_block), planes(block_diag), planes(block_inv)
    fields = [planes(a) for a in (weights, pivots, lower_ratio, upper_ratio)]

    def line(count):
        return (count, LANES)

    message, base, from_below, from_above, strengths, owners = call(
        sweep_kernel,
        "sweep",
        [ids, cells, perfs, index, krylov, *fields, diag, inv],
        [
            (line(CHUNKS * MSG), "vmem"),
            (line(COLS * PLANE), "vmem"),
            (line(PLANE), "vmem"),
            (line(PLANE), "vmem"),
            (line(8), "vmem"),
            (line(8), "vmem", jnp.int32),
        ],
        scratch=[line(6 * PLANE), (96, XS, LANES), (24, XS, LANES)]
        + [(8, XS, LANES)] * 3
        + [(24, XS, LANES)] * 2
        + [pltpu.SMEM((1, WELLS), jnp.int32), pltpu.VMEM((PERFS, WELLS), jnp.int32)]
        + [(PERFS, WELLS)],
        sems=21,
    )
    fixed, by_below, by_above, fixed_rows, by_below_rows, by_above_rows, columns = call(
        ahead_kernel,
        "ahead",
        [krylov, diag, inv, send_rows, (base, "vmem"), (from_below, "vmem"), (from_above, "vmem")],
        [
            (line(12 * PLANE), "hbm"),
            (line(3 * PLANE), "hbm"),
            (line(3 * PLANE), "hbm"),
            (line(TILES * 96), "vmem"),
            (line(TILES * 24), "vmem"),
            (line(TILES * 24), "vmem"),
            (line(TILES * SLOTS), "vmem"),
        ],
        scratch=[line(12 * PLANE), line(3 * PLANE), line(3 * PLANE)]
        + [(96, XS, LANES), (24, XS, LANES), (72, XS, LANES)]
        + [pltpu.SMEM((SLOTS, TILES), jnp.int32)],
        sems=14,
    )
    message = lax.all_to_all(
        message.reshape(CHUNKS, MSG, LANES), "layer", split_axis=0, concat_axis=0, tiled=True
    )
    (reply,) = call(
        chain_kernel,
        "chain",
        [(owners, "vmem"), (rows(message), "vmem")],
        [(line(CHUNKS * MSG), "vmem")],
        scratch=[(LANES, 2 * LANES)],
        sems=0,
    )
    reply = lax.all_to_all(
        reply.reshape(CHUNKS, MSG, LANES), "layer", split_axis=0, concat_axis=0, tiled=True
    )
    reply = rows(reply)
    (outgoing,) = call(
        outgoing_kernel,
        "outgoing",
        [
            (reply, "vmem"), (fixed_rows, "vmem"), (by_below_rows, "vmem"),
            (by_above_rows, "vmem"), (columns, "vmem"),
        ],
        [(line(TILES * 96), "hbm")],
        scratch=[line(TILES * 96)],
        sems=2,
    )
    arrived = lax.all_to_all(
        outgoing.reshape(TILES, 96, LANES), ("tx", "ty"), split_axis=0, concat_axis=0, tiled=True
    )
    precond, x_a, x_b, layer_a, layer_b, across, rates = call(
        precond_kernel,
        "precond",
        [ids, (reply, "vmem"), (fixed, "hbm"), (by_below, "hbm"), (by_above, "hbm")],
        [
            (line(12 * PLANE), "hbm"),
            (line(96), "hbm"),
            (line(96), "hbm"),
            ((12, XS, LANES), "hbm"),
            ((12, XS, LANES), "hbm"),
            (line(XS), "hbm"),
            (line(8), "vmem"),
        ],
        scratch=[line(12 * PLANE), line(96), line(96), line(XS)]
        + [line(12 * PLANE), line(3 * PLANE), line(3 * PLANE)],
        sems=15,
    )
    across = lax.ppermute(across, "ty", pairs(n_ty, False))
    x_a = lax.ppermute(x_a, "tx", pairs(n_tx, False))
    x_b = lax.ppermute(x_b, "tx", pairs(n_tx, True))
    layer_a = lax.ppermute(layer_a, "layer", pairs(n_layer, False))
    layer_b = lax.ppermute(layer_b, "layer", pairs(n_layer, True))
    devices = n_layer * n_tx * n_ty
    partial, edges, targets, coef = call(
        stencil_kernel,
        "stencil",
        [
            ids, cells, recv_rows, counts, (precond, "hbm"), (across, "hbm"), (rows(layer_a), "hbm"),
            (rows(layer_b), "hbm"), (rows(block_diag), "hbm"), (rows(face_coef), "hbm"),
            (rows(fault_coef), "hbm"), (rates, "vmem"), (strengths, "vmem"),
        ],
        [
            (line(12 * PLANE), "vmem"),
            (line(16), "vmem"),
            (line(PLANE), "vmem"),
            (line(TILES * SLOTS), "vmem"),
        ],
        scratch=[line(12 * PLANE), line(XS), line(12 * XS), line(12 * XS), line(9 * PLANE), line(6 * PLANE)]
        + [pltpu.SMEM((1, WELLS), jnp.int32), pltpu.SMEM((SLOTS, TILES), jnp.int32)]
        + [pltpu.SMEM((1, TILES), jnp.int32)],
        sems=10,
    )
    image, gram = call(
        finish_kernel,
        "finish",
        [
            ids, (partial, "vmem"), (x_a, "vmem"), (x_b, "vmem"), (arrived, "vmem"),
            (coef, "vmem"), (edges, "vmem"), (targets, "vmem"),
        ],
        [(line(12 * PLANE), "vmem"), (line(devices), "vmem")],
        sems=0,
        alias={1: 0},
    )
    gathered = lax.all_to_all(gram, ALL, split_axis=0, concat_axis=0, tiled=True)
    entries = float(12 * PLANE * LANES // COLS * devices)

    def factor(*refs):
        factor_kernel(1.0 / entries, *refs)

    q, r_factor = call(
        factor,
        "factor",
        [(gathered, "vmem"), (image, "vmem")],
        [((12, PLANE, LANES), "hbm"), ((COLS, COLS), "hbm")],
        scratch=[(12, PLANE, LANES), (COLS, COLS)],
        sems=5,
    )
    return (q.reshape(krylov_block.shape), r_factor)


def solution(mesh):
    placed = (
        P(None, None, "layer", "tx", "ty"),
        P(None, "layer", "tx", "ty"),
        P("layer", "tx", "ty"),
        P("layer", "tx", "ty"),
        P("layer", "tx", "ty"),
        P(None, "layer", "tx", "ty"),
        P(None, "layer", "tx", "ty"),
        P(None, "layer", "tx", "ty"),
        P("layer", "tx", "ty", None, None),
        P("layer", "tx", "ty", None, None),
        P("layer", "tx", "ty", None),
        P("layer", "tx", "ty", None, None, None),
        P("tx", "ty", None),
        P("tx", "ty", None, None),
        P("tx", "ty", None, None),
    )
    return jax.shard_map(
        on_device,
        mesh=mesh,
        in_specs=placed,
        out_specs=(P(None, None, "layer", "tx", "ty"), P()),
        check_vma=False,
    )
```
